128 devices in a mesh: branch: 2 (over core), section: 2 (over z_hi), patch: 32 (over z_lo, y, x).
Axes of the slice: x: 4, y: 4, z: 4 (z_hi: 2, z_lo: 2; z = z_hi * 2 + z_lo), core: 2. Of those that a mesh axis runs over, the one named last changes fastest.
Arguments:
- stream: bfloat16 [3840, 2560], P('patch'), may hold values from -6 to 6
- token_frame: int32 [3840], P('patch'), may hold values from 0 to 15, never falling along the last dimension, each value on 1 to 480 neighbouring positions
- frame_levels: int32 [16], replicated, may hold values from 0 to 49
- level_table: float32 [50, 7680], replicated, may hold values from -3 to 3
- branch_mod: float32 [2, 7680], P('branch'), may hold values from -2.4 to 2.4
- layer_mod: float32 [2, 7680], P('section'), may hold values from -1.8 to 1.8
- maps: float32 [2, 3, 2560], P('section'), may hold values from -3.6 to 3.6
- stale_kv: bfloat16 [2, 2, 2, 3840, 2560], P('branch', 'section', None, 'patch'), may hold values from -204 to 204
Outputs:
- guided: bfloat16 [3840, 2560], P('patch', 'branch')
- fresh_kv: bfloat16 [2, 2, 2, 3840, 2560], P('branch', 'section', None, 'patch')
The draws below stay inside these ranges and needn't reach their ends.
Inputs may be any that keep to these rules, and one draw needn't show every extreme that they name: token_frame never falls from one token to the next, and every frame holds between 1 and 480 tokens.
All inputs are finite; a program needn't handle non-finite values.
Results may differ from the reference program's by a relative error of at most 0.025.
Values may be sent and summed in bfloat16 or wider, within the bound.
No kernel may reach another device: no remote copies, remote signals or barrier semaphores. Data moves between devices by JAX's collectives and lax.ppermute only.
A program may use at most 256 MiB of HBM per device.

```python
import math
import jax
import jax.numpy as jnp
import numpy as np
from jax import lax

HEADS = 20
HEAD_DIM = 128
TOK_DEV = 120
FRAMES = 16
LEVELS = 50
CHANNELS = 2560
TOKENS = 3840
SECTIONS = 2
BRANCHES = 2


def draw_stale_kv(key, part):
    key = jax.random.fold_in(key, 7)
    first = jax.random.fold_in(key, 0)
    extent = (BRANCHES, SECTIONS, 2, TOKENS, HEADS * HEAD_DIM)
    base = jnp.clip(jax.random.normal(first, extent, jnp.float32), -6.0, 6.0)
    return base.astype(jnp.bfloat16)


def with_ends(values, own_key, smallest, top_value):
    spot = [jax.random.randint(jax.random.fold_in(own_key, axis), (), 0, length) for axis, length in enumerate(values.shape)]
    longest = values.shape.index(max(values.shape))
    next_to = spot[:longest] + [(spot[longest] + 1) % values.shape[longest]] + spot[longest + 1:]
    return values.at[tuple(spot)].set(smallest).at[tuple(next_to)].set(top_value)


def level_of(rng, dims, shards, least, top_value):
    loudness, own = 1.0, jax.random.fold_in(rng, 6)
    for position, parts in shards:
        heights = jnp.exp(jax.random.uniform(jax.random.fold_in(own, position), (parts,), jnp.float32, least / len(shards), top_value / len(shards)))
        loudness = loudness * jnp.repeat(heights, dims[position] // parts).reshape([-1 if axis == position else 1 for axis in range(len(dims))])
    return loudness


def split_up(count, total, bound, slope):
    portions = [(1 << 20) // math.isqrt(rank ** slope) + 1 for rank in range(2, count + 1)]
    surplus, counts = total - bound - (count - 1), [1] * (count - 1)
    while surplus > 0:
        free = [i for i in range(count - 1) if counts[i] < bound]
        pool, remaining = sum([portions[i] for i in free]), surplus
        for i in free:
            extra = min(bound - counts[i], max(1, remaining * portions[i] // pool), surplus)
            counts[i] = counts[i] + extra
            surplus = surplus - extra
    return np.array([bound] + counts)


def uneven(key, count, total, reach, skew):
    if count == 2:
        one = jax.random.randint(key, (), max(1, total - reach), min(reach, total - 1) + 1)
        return jnp.stack([one, total - one])
    lengths = jnp.asarray(split_up(count, total, reach, skew), jnp.int32)
    couples = (count - 1) // 2
    donor, receiver = lengths[1:1 + 2 * couples:2], lengths[2:2 + 2 * couples:2]
    slack = jnp.minimum(donor - 1, reach - receiver)
    shifted = jax.random.randint(jax.random.fold_in(key, 1), (couples,), 0, 1 << 20) % (slack + 1)
    lengths = lengths.at[1:1 + 2 * couples:2].set(donor - shifted).at[2:2 + 2 * couples:2].set(receiver + shifted)
    return lengths[jax.random.permutation(jax.random.fold_in(key, 2), count)]


def normal_values(own_key, dims, deviation, reach, cuts=(), kind=jnp.bfloat16):
    loudness = level_of(own_key, dims, cuts, -0.22, 0.18) if cuts else 1.0
    entries = jax.random.normal(own_key, dims, jnp.float32) * deviation * loudness
    return jnp.minimum(jnp.maximum(entries, -reach), reach).astype(kind)


def setup_inputs(seed: int = 0) -> dict:
    seeds = jax.random.split(jax.random.key(seed), 9)
    stream = normal_values(seeds[0], (TOKENS, CHANNELS), 1.0, 6.0, ((0, 32),))
    token_frame = jnp.searchsorted(jnp.cumsum(uneven(seeds[1], FRAMES, TOKENS, TOKENS // 8, 1)), jnp.arange(TOKENS), side="right").astype(jnp.int32)
    frame_levels = with_ends(jax.random.randint(seeds[2], (FRAMES,), 0, LEVELS), jax.random.fold_in(seeds[2], 1), 0, LEVELS - 1).astype(jnp.int32)
    level_table = normal_values(seeds[3], (LEVELS, 3 * CHANNELS), 0.5, 3.0, (), jnp.float32)
    branch_mod = normal_values(seeds[4], (BRANCHES, 3 * CHANNELS), 0.4, 2.4, ((0, 2),), jnp.float32)
    layer_mod = normal_values(seeds[5], (SECTIONS, 3 * CHANNELS), 0.3, 1.8, ((0, 2),), jnp.float32)
    maps = normal_values(seeds[6], (SECTIONS, 3, CHANNELS), 0.6, 3.6, ((0, 2),), jnp.float32)
    stale_kv = draw_stale_kv(jax.random.fold_in(seeds[8], 71), 0)
    return {"stream": stream, "token_frame": token_frame, "frame_levels": frame_levels, "level_table": level_table, "branch_mod": branch_mod, "layer_mod": layer_mod, "maps": maps, "stale_kv": stale_kv}


EPSILON = 1e-06
GUIDE = 5.0

def attend(query, keys_fresh, values_fresh, keys_stale, values_stale, same):
    factor = HEAD_DIM ** (-0.5)

    def split_heads(array):
        return array.reshape(TOKENS, HEADS, HEAD_DIM).transpose(1, 0, 2)

    def one_head(items):
        query_head, fresh_k, fresh_v, stale_k, stale_v = items
        fresh_scores = jnp.dot(query_head, fresh_k.T, preferred_element_type=jnp.float32) * factor
        stale_scores = jnp.dot(query_head, stale_k.T, preferred_element_type=jnp.float32) * factor
        scores = jnp.where(same, fresh_scores, stale_scores)
        peak = lax.optimization_barrier(jnp.max(scores, axis=1, keepdims=True))
        powers = jnp.exp(scores - peak)
        total = lax.optimization_barrier(jnp.sum(powers, axis=1))
        weights = powers.astype(jnp.bfloat16)
        nothing = jnp.zeros((), jnp.bfloat16)
        summed = jnp.dot(jnp.where(same, weights, nothing), fresh_v, preferred_element_type=jnp.float32)
        summed = summed + jnp.dot(jnp.where(same, nothing, weights), stale_v, preferred_element_type=jnp.float32)
        return summed / total[:, None]
    result = lax.map(one_head, (split_heads(query), split_heads(keys_fresh), split_heads(values_fresh), split_heads(keys_stale), split_heads(values_stale)))
    return result.transpose(1, 0, 2).reshape(TOKENS, HEADS * HEAD_DIM)

def layer(current, modulation, gains, keys_stale, values_stale, same):
    width = current.shape[1]
    shift_term = modulation[:, :width]
    scaling = modulation[:, width:2 * width]
    gate_term = modulation[:, 2 * width:]
    values_in = current.astype(jnp.float32)
    normed = values_in * lax.rsqrt(lax.optimization_barrier(jnp.mean(values_in * values_in, axis=1, keepdims=True)) + EPSILON)
    hidden = normed * (1.0 + scaling) + shift_term
    query = (hidden * gains[0]).astype(jnp.bfloat16)
    fresh_keys = (hidden * gains[1]).astype(jnp.bfloat16)
    fresh_values = (hidden * gains[2]).astype(jnp.bfloat16)
    attended = attend(query, fresh_keys, fresh_values, keys_stale, values_stale, same)
    result = (values_in + gate_term * attended).astype(jnp.bfloat16)
    return (result, fresh_keys, fresh_values)

def reference(stream, token_frame, frame_levels, level_table, branch_mod, layer_mod, maps, stale_kv):
    base = level_table[frame_levels[token_frame]]
    patch_ids = jnp.arange(TOKENS, dtype=jnp.int32) // TOK_DEV
    same = patch_ids[:, None] == patch_ids[None, :]
    finals = []
    fresh_all = []
    for branch_no in range(BRANCHES):
        current = stream
        fresh_layers = []
        for layer_no in range(SECTIONS):
            modulation = base + (layer_mod[layer_no] + branch_mod[branch_no])[None, :]
            current, fresh_keys, fresh_values = layer(current, modulation, maps[layer_no], stale_kv[branch_no, layer_no, 0], stale_kv[branch_no, layer_no, 1], same)
            fresh_layers.append(jnp.stack([fresh_keys, fresh_values]))
        finals.append(current)
        fresh_all.append(jnp.stack(fresh_layers))
    cond_out = finals[0].astype(jnp.float32)
    uncond_out = finals[1].astype(jnp.float32)
    guided = (uncond_out + GUIDE * (cond_out - uncond_out)).astype(jnp.bfloat16)
    return (guided, jnp.stack(fresh_all))
```

```python
import functools
import math

import jax
import jax.numpy as jnp
from jax import lax
from jax.experimental import pallas as pl
from jax.experimental.pallas import tpu as pltpu
from jax.sharding import PartitionSpec as P

HEADS = 20
HEAD_DIM = 128
FRAMES = 16
LEVELS = 50
TOK = 120
THIRD = 40
PATCHES = 32
WIDTH = HEADS * HEAD_DIM
EPSILON = 1e-06
GUIDE = 5.0
BIG = 1e30
PLANE = ("section", "patch")
F32 = jnp.float32
BF16 = jnp.bfloat16
VMEM_BYTES = 56 * 1024 * 1024
PARAMS = pltpu.CompilerParams(vmem_limit_bytes=VMEM_BYTES)

OWN_ROWS = PATCHES * THIRD
TILE = 4 * THIRD
CHUNK = 320
MID = 64


def place_of(head, third):
    if head < 16:
        return 4 * head + third
    return 16 * (head - 16) + 4 * third + 3


def dot(a, b, dims):
    return lax.dot_general(a, b, (dims, ((), ())), preferred_element_type=F32)


NN = ((1,), (0,))
NT = ((1,), (1,))
TN = ((0,), (0,))


def split3(v):
    hi = v.astype(BF16).astype(F32)
    mid = (v - hi).astype(BF16).astype(F32)
    low = (v - hi - mid).astype(BF16).astype(F32)
    return hi, mid, low


def turned(rows, third):
    cut = THIRD * third
    return rows if cut == 0 else jnp.concatenate([rows[cut:TOK], rows[:cut]], axis=0)


def pack_kernel(scal, kv, kv_more, x, x_more, stream, frames, out, aux):
    step = pl.program_id(0)
    section = scal[0]

    @pl.when(step == 0)
    def _():
        values = stream[...].astype(F32)
        square = values * values
        ones = jnp.ones((8, WIDTH), BF16)
        row = lax.broadcasted_iota(jnp.int32, (8, 128), 0)
        lane = lax.broadcasted_iota(jnp.int32, (8, 128), 1)
        for third in range(3):
            t = jnp.concatenate([turned(square, third), jnp.zeros((8, WIDTH), F32)], axis=0)
            hi = t.astype(BF16)
            low = (t - hi.astype(F32)).astype(BF16)
            total = dot(ones, hi, NT) + dot(ones, low, NT)
            r = jnp.where(lane < TOK, lax.rsqrt(total * (1.0 / WIDTH) + EPSILON), 0.0)
            hi, mid, low = split3(r)
            a = jnp.where(row == 0, hi, jnp.where(row == 1, mid, jnp.where(row == 2, low, 0.0)))
            aux[third] = jnp.where(row == 3, frames[third : third + 1, :], a)

    def halves(block):
        values = block[...].astype(F32)
        parts = []
        for third in range(3):
            t = turned(values, third)
            parts.append(jnp.where(section == 0, t[0:64], t[TOK - 64 : TOK]))
        return parts

    none = jnp.zeros((8, 128), F32)
    keys = kv[0].astype(F32)
    vals = jnp.concatenate([kv[1].astype(F32), none], axis=0).astype(BF16)
    xs = halves(x)
    for third in range(3):
        out[third, 0:128] = jnp.concatenate([keys, aux[third]], axis=0).astype(BF16)
        out[third, 128:256] = vals
        out[third, 256:CHUNK] = xs[third].astype(BF16)
    y = lax.rem(step, 4)
    keys = kv_more[0].astype(F32)
    vals = jnp.concatenate([kv_more[1].astype(F32), none], axis=0).astype(BF16)
    xs = halves(x_more)
    which = jnp.where(y == 3, 0, y)
    out[3, 0:128] = jnp.concatenate([keys, aux[which]], axis=0).astype(BF16)
    out[3, 128:256] = vals
    chosen = jnp.where(which == 0, xs[0], jnp.where(which == 1, xs[1], xs[2]))
    out[3, 256:CHUNK] = chosen.astype(BF16)


def pack(section, stale, stream, frames):
    grid = pltpu.PrefetchScalarGridSpec(
        num_scalar_prefetch=1,
        grid=(16,),
        in_specs=[
            pl.BlockSpec((2, TOK, 128), lambda r, s: (0, 0, r)),
            pl.BlockSpec((2, TOK, 128), lambda r, s: (0, 0, 16 + r // 4)),
            pl.BlockSpec((TOK, 128), lambda r, s: (0, r)),
            pl.BlockSpec((TOK, 128), lambda r, s: (0, 16 + r // 4)),
            pl.BlockSpec((TOK, WIDTH), lambda r, s: (0, 0)),
            pl.BlockSpec((8, 128), lambda r, s: (0, 0)),
        ],
        out_specs=pl.BlockSpec((4, CHUNK, 128), lambda r, s: (r, 0, 0)),
        scratch_shapes=[pltpu.VMEM((3, 8, 128), F32)],
    )
    return pl.pallas_call(
        pack_kernel,
        grid_spec=grid,
        out_shape=jax.ShapeDtypeStruct((64, CHUNK, 128), BF16),
        compiler_params=PARAMS,
        name="pack",
    )(section, stale, stale, stream, stream, stream, frames)


def mod_table(frame_mod, with_scale):
    hi, mid, low = split3(frame_mod)
    table = jnp.concatenate([hi, mid, low, jnp.zeros((16, frame_mod.shape[1]), F32)], axis=0)
    if with_scale:
        row = lax.broadcasted_iota(jnp.int32, (64, 128), 0)
        extra = jnp.where((row >= 48) & (row < 51), 1.0, 0.0)
        table = jnp.concatenate([table, extra], axis=1)
    return table.astype(BF16)


def hot_rows(aux):
    row = lax.broadcasted_iota(jnp.int32, (48, 128), 0)
    hot = jnp.where((row & 15).astype(F32) == aux[3:4, :], 1.0, 0.0)
    return jnp.concatenate([hot, aux, jnp.zeros((8, 128), F32)], axis=0).astype(BF16)


def place_keys(p, kv, ka, va):
    row = lax.broadcasted_iota(jnp.int32, (128, 128), 0)
    col = lax.broadcasted_iota(jnp.int32, (128, 128), 1)
    at = pl.ds(pl.multiple_of(p * 128, 128), 128)
    hidden = (col == p) | ((col == PATCHES) & (row >= TOK))
    ka[at, 0:128] = kv[0, p, 0:128, :]
    ka[at, 128:256] = jnp.where(hidden, -BIG, 0.0).astype(BF16)
    va[at, 0:128] = kv[0, p, 128:256, :]
    va[at, 128:256] = jnp.ones((128, 128), BF16)


def place_fresh(p, hid, maps, fk, fv):
    row = lax.broadcasted_iota(jnp.int32, (128, 128), 0)
    col = lax.broadcasted_iota(jnp.int32, (128, 128), 1)
    at = pl.ds(pl.multiple_of(p * 128, 128), 128)
    fk[at, 0:128] = (hid * maps[1:2, :]).astype(BF16)
    fk[at, 128:256] = jnp.where((col == PATCHES) & (row >= TOK), -BIG, 0.0).astype(BF16)
    fv[at, 0:128] = (hid * maps[2:3, :]).astype(BF16)
    fv[at, 128:256] = jnp.ones((128, 128), BF16)


def place_query(t, pair_hid, maps, qa):
    row = lax.broadcasted_iota(jnp.int32, (80, 128), 0)
    col = lax.broadcasted_iota(jnp.int32, (80, 128), 1)
    patch = 2 * t + jnp.where(row >= THIRD, 1, 0)
    at = pl.ds(pl.multiple_of(t * 80, 16), 80)
    qa[at, 0:128] = (pair_hid * maps[0:1, :]).astype(BF16)
    qa[at, 128:256] = jnp.where((col == patch) | (col == PATCHES), 1.0, 0.0).astype(BF16)


def attention(qa, ka, va, fk, fv, xo, go, sc, pc, result):
    factor = HEAD_DIM ** (-0.5) * math.log2(math.e)
    keys = ka.shape[0]
    step = 512

    @pl.loop(0, OWN_ROWS // TILE)
    def _(tile):
        at = pl.ds(pl.multiple_of(tile * TILE, 16), TILE)
        q = qa[at, :]
        top = None
        for begin in range(0, keys, step):
            s = dot(q, ka[begin : begin + step, :], NT)
            sc[:, begin : begin + step] = s
            for lane in range(0, step, 128):
                part = s[:, lane : lane + 128]
                top = part if top is None else jnp.maximum(top, part)
        fresh = []
        for pair in range(2):
            low = pl.multiple_of(tile * TILE + pair * 80, 16)
            klow = pl.multiple_of((tile * 4 + pair * 2) * 128, 256)
            s = dot(qa[pl.ds(low, 80), :], fk[pl.ds(klow, 256), :], NT)
            fresh.append(s[0:THIRD, 0:128])
            fresh.append(s[THIRD:80, 128:256])
        fresh = jnp.concatenate(fresh, axis=0)
        top = jnp.max(jnp.maximum(top, fresh), axis=1, keepdims=True)
        for begin in range(0, keys, step):
            pc[:, begin : begin + step] = jnp.exp2((sc[:, begin : begin + step] - top) * factor).astype(BF16)
        total = dot(pc[...], va[...], NN)
        power = jnp.exp2((fresh - top) * factor)
        none = jnp.zeros((THIRD, 128), F32)
        added = []
        for pair in range(2):
            a = power[pair * 80 : pair * 80 + THIRD]
            b = power[pair * 80 + THIRD : pair * 80 + 80]
            both = jnp.concatenate(
                [jnp.concatenate([a, none], axis=1), jnp.concatenate([none, b], axis=1)], axis=0
            ).astype(BF16)
            klow = pl.multiple_of((tile * 4 + pair * 2) * 128, 256)
            added.append(dot(both, fv[pl.ds(klow, 256), :], NN))
        total = total + jnp.concatenate(added, axis=0)
        attended = total[:, 0:128] / total[:, 128:256]
        result(at, (xo[at, :] + go[at, :] * attended).astype(BF16))


def first_kernel(kv, x_rest, frame_mod, maps, x_out, mid, qa, ka, va, fk, fv, xo, go, sc, pc, sq):
    table = mod_table(frame_mod[...], True)
    gains = maps[...]

    @pl.loop(0, 4)
    def _(block):
        for sub in range(4):
            t = block * 4 + sub
            hids, xs, gates = [], [], []
            for half in range(2):
                p = 2 * t + half
                aux = kv[0, p, 112:128, :].astype(F32)[8:16]
                xa = kv[0, p, 256:CHUNK, :].astype(F32)
                xb = x_rest[0, p].astype(F32)[8:64]
                x = jnp.concatenate([xa, xb, jnp.zeros((8, 128), F32)], axis=0)
                m = dot(hot_rows(aux), table, TN)
                hid = x * m[:, 384:512] * (1.0 + m[:, 128:256]) + m[:, 0:128]
                place_keys(p, kv, ka, va)
                place_fresh(p, hid, gains, fk, fv)
                hids.append(hid[0:THIRD])
                xs.append(x[0:THIRD])
                gates.append(m[0:THIRD, 256:384])
            place_query(t, jnp.concatenate(hids, axis=0), gains, qa)
            at = pl.ds(pl.multiple_of(t * 80, 16), 80)
            xo[at, :] = jnp.concatenate(xs, axis=0)
            go[at, :] = jnp.concatenate(gates, axis=0)

    def result(at, value):
        x_out[at, :] = value
        wide = value.astype(F32)
        sq[at, :] = wide * wide

    attention(qa, ka, va, fk, fv, xo, go, sc, pc, result)
    square = sq[...]
    hi = square.astype(BF16)
    low = (square - hi.astype(F32)).astype(BF16)
    ones = jnp.ones((8, 128), BF16)
    total = dot(ones, hi, NT) + dot(ones, low, NT)
    hi = total.astype(BF16).astype(F32)
    low = total - hi
    rows = [part[0:1, 128 * i : 128 * i + 128] for part in (hi, low) for i in range(10)]
    sums = jnp.concatenate(rows + [jnp.zeros((4, 128), F32)], axis=0)
    for t in range(PATCHES // 2):
        pair = x_out[80 * t : 80 * t + 80, :].astype(F32)
        for half in range(2):
            p = 2 * t + half
            block = jnp.concatenate([pair[THIRD * half : THIRD * half + THIRD], sums], axis=0).astype(BF16)
            mid[p] = block
            mid[PATCHES + p] = block


SCRATCH = [
    pltpu.VMEM((OWN_ROWS, 256), BF16),
    pltpu.VMEM((PATCHES * 128, 256), BF16),
    pltpu.VMEM((PATCHES * 128, 256), BF16),
    pltpu.VMEM((PATCHES * 128, 256), BF16),
    pltpu.VMEM((PATCHES * 128, 256), BF16),
    pltpu.VMEM((OWN_ROWS, 128), F32),
    pltpu.VMEM((OWN_ROWS, 128), F32),
    pltpu.VMEM((TILE, PATCHES * 128), F32),
    pltpu.VMEM((TILE, PATCHES * 128), BF16),
]


def first_layer(received, frame_mod, maps):
    return pl.pallas_call(
        first_kernel,
        grid=(1,),
        in_specs=[
            pl.BlockSpec((1, PATCHES, CHUNK, 128), lambda i: (0, 0, 0, 0)),
            pl.BlockSpec((1, PATCHES, 64, 128), lambda i: (1, 0, 4, 0)),
            pl.BlockSpec((16, 384), lambda i: (0, 0)),
            pl.BlockSpec((3, 128), lambda i: (0, 0)),
        ],
        out_specs=[
            pl.BlockSpec((OWN_ROWS, 128), lambda i: (0, 0)),
            pl.BlockSpec((64, MID, 128), lambda i: (0, 0, 0)),
        ],
        out_shape=[
            jax.ShapeDtypeStruct((OWN_ROWS, 128), BF16),
            jax.ShapeDtypeStruct((64, MID, 128), BF16),
        ],
        scratch_shapes=SCRATCH + [pltpu.VMEM((OWN_ROWS, 128), F32)],
        compiler_params=PARAMS,
        name="first_layer",
    )(received, received, frame_mod, maps)


def second_kernel(scal, kv, own, after, before, sums, frame_mod, maps, x_out, qa, ka, va, fk, fv, xo, go, sc, pc, rs):
    table = mod_table(frame_mod[...], False)
    gains = maps[...]
    third = scal[0]
    row = lax.broadcasted_iota(jnp.int32, (16, OWN_ROWS), 0)
    ones = jnp.where(lax.broadcasted_iota(jnp.int32, (16, 128), 0) < 3, 1.0, 0.0).astype(BF16)
    for k in range(3):
        which = lax.rem(third + k, 3)
        total = None
        for head in range(HEADS):
            at = 4 * head + which if head < 16 else 16 * (head - 16) + 4 * which + 3
            part = sums[at].astype(F32)
            total = part if total is None else total + part
        square = jnp.concatenate([total[8 + i : 9 + i] + total[18 + i : 19 + i] for i in range(10)], axis=1)
        hi, mid, low = split3(lax.rsqrt(square * (1.0 / WIDTH) + EPSILON))
        r = jnp.where(row == 0, hi, jnp.where(row == 1, mid, jnp.where(row == 2, low, 0.0)))
        rs[k] = dot(r.astype(BF16), ones, TN)

    @pl.loop(0, 4)
    def _(block):
        for sub in range(4):
            t = block * 4 + sub
            at = pl.ds(pl.multiple_of(t * 80, 16), 80)
            pair = [ref[at, :].astype(F32) for ref in (own, after, before)]
            scale = [rs[k, at, :] for k in range(3)]
            hids, gates = [], []
            for half in range(2):
                p = 2 * t + half
                cut = slice(THIRD * half, THIRD * half + THIRD)
                aux = kv[0, p, 112:128, :].astype(F32)[8:16]
                none = [jnp.zeros((8, 128), F32)]
                x = jnp.concatenate([v[cut] for v in pair] + none, axis=0)
                r = jnp.concatenate([v[cut] for v in scale] + none, axis=0)
                m = dot(hot_rows(aux), table, TN)
                hid = x * r * (1.0 + m[:, 128:256]) + m[:, 0:128]
                place_keys(p, kv, ka, va)
                place_fresh(p, hid, gains, fk, fv)
                hids.append(hid[0:THIRD])
                gates.append(m[0:THIRD, 256:384])
            place_query(t, jnp.concatenate(hids, axis=0), gains, qa)
            xo[at, :] = pair[0]
            go[at, :] = jnp.concatenate(gates, axis=0)

    def result(at, value):
        x_out[at, :] = value

    attention(qa, ka, va, fk, fv, xo, go, sc, pc, result)


def second_layer(third, received, own, after, before, sums, frame_mod, maps):
    rows = pl.BlockSpec((OWN_ROWS, 128), lambda i, s: (0, 0))
    grid = pltpu.PrefetchScalarGridSpec(
        num_scalar_prefetch=1,
        grid=(1,),
        in_specs=[
            pl.BlockSpec((1, PATCHES, 256, 128), lambda i, s: (1, 0, 0, 0)),
            rows,
            rows,
            rows,
            pl.BlockSpec((64, 32, 128), lambda i, s: (0, 1, 0)),
            pl.BlockSpec((16, 384), lambda i, s: (0, 0)),
            pl.BlockSpec((3, 128), lambda i, s: (0, 0)),
        ],
        out_specs=rows,
        scratch_shapes=SCRATCH + [pltpu.VMEM((3, OWN_ROWS, 128), F32)],
    )
    return pl.pallas_call(
        second_kernel,
        grid_spec=grid,
        out_shape=jax.ShapeDtypeStruct((OWN_ROWS, 128), BF16),
        compiler_params=PARAMS,
        name="second_layer",
    )(third, received, own, after, before, sums, frame_mod, maps)


def home_kernel(scal, got, stream, frames, frame_mod, maps, out, xs):
    section = scal[0]
    square = jnp.zeros((TOK, 128), F32)
    for head in range(HEADS):
        cols = slice(128 * head, 128 * head + 128)
        parts = [got[place_of(head, third)].astype(F32)[0:THIRD] for third in range(3)]
        x = jnp.where(section == 0, stream[:, cols].astype(F32), jnp.concatenate(parts, axis=0))
        xs[:, cols] = x
        square = square + x * x
    r = lax.rsqrt(jnp.sum(square, axis=1, keepdims=True) * (1.0 / WIDTH) + EPSILON)
    row = lax.broadcasted_iota(jnp.int32, (48, 128), 0)
    hot = jnp.where((row & 15).astype(F32) == frames[0:1, :], 1.0, 0.0).astype(BF16)
    for head in range(HEADS):
        cols = slice(128 * head, 128 * head + 128)
        more = slice(WIDTH + 128 * head, WIDTH + 128 * head + 128)
        mod = jnp.concatenate([frame_mod[:, cols], frame_mod[:, more]], axis=1)
        m = dot(hot, jnp.concatenate(split3(mod), axis=0).astype(BF16), TN)[0:TOK]
        hid = xs[:, cols] * r * (1.0 + m[:, 128:256]) + m[:, 0:128]
        out[0, :, cols] = (hid * maps[1:2, cols]).astype(BF16)
        out[1, :, cols] = (hid * maps[2:3, cols]).astype(BF16)


def home(section, got, stream, frames, frame_mod, maps):
    whole = pl.BlockSpec(memory_space=pltpu.VMEM)
    return pl.pallas_call(
        home_kernel,
        in_specs=[pl.BlockSpec(memory_space=pltpu.SMEM)] + [whole] * 5,
        out_specs=whole,
        out_shape=jax.ShapeDtypeStruct((2, TOK, WIDTH), BF16),
        scratch_shapes=[pltpu.VMEM((TOK, WIDTH), F32)],
        compiler_params=PARAMS,
        name="home",
    )(section, got, stream, frames, frame_mod, maps)


def unpack_kernel(scal, got, out):
    branch = scal[0]
    for j in range(HEADS // 2):
        parts = []
        for third in range(3):
            a, b = place_of(j, third), place_of(j + HEADS // 2, third)
            parts.append(got[jnp.where(branch == 0, a, b)].astype(F32))
        out[:, 128 * j : 128 * j + 128] = jnp.concatenate(parts, axis=0).astype(BF16)


def unpack(branch, got):
    whole = pl.BlockSpec(memory_space=pltpu.VMEM)
    return pl.pallas_call(
        unpack_kernel,
        in_specs=[pl.BlockSpec(memory_space=pltpu.SMEM), whole],
        out_specs=whole,
        out_shape=jax.ShapeDtypeStruct((TOK, WIDTH // 2), BF16),
        compiler_params=PARAMS,
        name="unpack",
    )(branch, got)


def body(stream, token_frame, frame_levels, level_table, branch_mod, layer_mod, maps, stale_kv):
    section = lax.axis_index("section")
    branch = lax.axis_index("branch")
    place = section * PATCHES + lax.axis_index("patch")
    x, y, z = place % 4, (place // 4) % 4, place // 16
    head = jnp.where(x < 3, place // 4, 16 + z)
    third = jnp.where(x < 3, x, jnp.where(y < 3, y, 0))

    both = jnp.concatenate([layer_mod.reshape(3, WIDTH), maps[0]], axis=0)
    other = lax.ppermute(both, "section", [(0, 1), (1, 0)])

    tf = token_frame.astype(F32)
    frames = jnp.stack([jnp.pad(jnp.roll(tf, -THIRD * k), (0, 8), constant_values=-1.0) for k in range(3)])
    frames = jnp.pad(frames, ((0, 5), (0, 0)))
    section_at = section.reshape(1).astype(jnp.int32)
    send = pack(section_at, stale_kv[0, 0], stream, frames)
    received = lax.all_to_all(send, PLANE, 0, 0, tiled=True)
    received = received.reshape(2, PATCHES, CHUNK, 128)

    level_hot = (frame_levels[:, None] == jnp.arange(LEVELS, dtype=jnp.int32)[None, :]).astype(F32)
    base = jnp.dot(level_hot, level_table, precision=lax.Precision.HIGHEST, preferred_element_type=F32)
    home_mod = base + (layer_mod[0] + branch_mod[0])[None, :]

    def of_head(array):
        rows = array.shape[0]
        return lax.dynamic_slice_in_dim(array.reshape(rows, -1, HEADS, 128), head, 1, 2)[:, :, 0]

    layers = jnp.stack([jnp.where(section == 0, both, other), jnp.where(section == 0, other, both)])
    mine = of_head(layers.reshape(12, WIDTH)).reshape(2, 6, 128)
    base_mine = of_head(base)
    branch_mine = of_head(branch_mod)[0]
    mods = base_mine[None] + (mine[:, 0:3] + branch_mine[None])[:, None]
    mods = mods.reshape(2, FRAMES, 384)
    gains = mine[:, 3:6]

    x_one, mid = first_layer(received, mods[0], gains[0])

    def from_third(by):
        pairs = [(place_of(h, (g + by) % 3), place_of(h, g)) for h in range(HEADS) for g in range(3)]
        return lax.ppermute(x_one, PLANE, pairs)

    after, before = from_third(1), from_third(2)
    mid_got = lax.all_to_all(mid, PLANE, 0, 0, tiled=True)
    fresh = home(section_at, mid_got, stream, frames, home_mod, maps[0])
    x_two = second_layer(third.reshape(1).astype(jnp.int32), received, x_one, after, before, mid_got, mods[1], gains[1])

    x_other = lax.ppermute(x_two, "branch", [(0, 1), (1, 0)])
    cond = jnp.where(branch == 0, x_two, x_other).astype(F32)
    uncond = jnp.where(branch == 0, x_other, x_two).astype(F32)
    guided = (uncond + GUIDE * (cond - uncond)).astype(BF16).reshape(1, PATCHES, THIRD, 128)
    guided = jnp.broadcast_to(guided, (2, PATCHES, THIRD, 128)).reshape(64, THIRD, 128)
    guided_got = lax.all_to_all(guided, PLANE, 0, 0, tiled=True)
    out = unpack(branch.reshape(1).astype(jnp.int32), guided_got)
    return (out, fresh[None, None])


def solution(mesh):
    placed = (
        P("patch", None),
        P("patch"),
        P(),
        P(),
        P("branch", None),
        P("section", None),
        P("section", None, None),
        P("branch", "section", None, "patch", None),
    )
    return jax.shard_map(
        body,
        mesh=mesh,
        in_specs=placed,
        out_specs=(P("patch", "branch"), P("branch", "section", None, "patch", None)),
        check_vma=False,
    )
```

```python
import functools
import math

import jax
import jax.numpy as jnp
from jax import lax
from jax.experimental import pallas as pl
from jax.experimental.pallas import tpu as pltpu
from jax.sharding import PartitionSpec as P

HEADS = 20
HEAD_DIM = 128
FRAMES = 16
LEVELS = 50
TOK = 120
THIRD = 40
PATCHES = 32
WIDTH = HEADS * HEAD_DIM
EPSILON = 1e-06
GUIDE = 5.0
BIG = 1e30
PLANE = ("section", "patch")
F32 = jnp.float32
BF16 = jnp.bfloat16
VMEM_BYTES = 56 * 1024 * 1024
PARAMS = pltpu.CompilerParams(vmem_limit_bytes=VMEM_BYTES)

OWN_ROWS = PATCHES * THIRD
TILE = 640
FACTOR = HEAD_DIM ** (-0.5) * math.log2(math.e)
CHUNK = 320
MID = 64


def place_of(head, third):
    if head < 16:
        return 4 * head + third
    return 16 * (head - 16) + 4 * third + 3


def dot(a, b, dims):
    return lax.dot_general(a, b, (dims, ((), ())), preferred_element_type=F32)


NN = ((1,), (0,))
NT = ((1,), (1,))
TN = ((0,), (0,))


def split3(v):
    hi = v.astype(BF16).astype(F32)
    mid = (v - hi).astype(BF16).astype(F32)
    low = (v - hi - mid).astype(BF16).astype(F32)
    return hi, mid, low


def turned(rows, third):
    cut = THIRD * third
    return rows if cut == 0 else jnp.concatenate([rows[cut:TOK], rows[:cut]], axis=0)


def pack_kernel(scal, stale, stream, frames, out, aux, frame_row):
    step = pl.program_id(0)
    section = scal[0]

    @pl.when(step == 0)
    def _():
        frame_row[...] = jnp.zeros((8, 128), F32)
        frame_row[0:1, 0:TOK] = frames[...].astype(F32)
        square = jnp.zeros((TOK, 128), F32)
        for head in range(HEADS):
            part = stream[:, 128 * head : 128 * head + 128].astype(F32)
            square = square + part * part
        square = jnp.concatenate([square, jnp.zeros((8, 128), F32)], axis=0)
        total = jnp.sum(square.T, axis=0, keepdims=True)
        r = lax.rsqrt(total * (1.0 / WIDTH) + EPSILON)
        hi, mid, low = split3(jnp.broadcast_to(r, (8, 128)))
        row = lax.broadcasted_iota(jnp.int32, (8, 128), 0)
        lane = lax.broadcasted_iota(jnp.int32, (8, 128), 1)
        a = jnp.where(row == 0, hi, jnp.where(row == 1, mid, jnp.where(row == 2, low, 0.0)))
        a = jnp.where(row == 3, frame_row[0:1, :], a)
        a = jnp.where(lane < TOK, a, 0.0)
        aux[0] = a
        for third in range(1, 3):
            cut = THIRD * third
            t = jnp.where(lane < TOK - cut, pltpu.roll(a, 128 - cut, 1), pltpu.roll(a, TOK - cut, 1))
            aux[third] = jnp.where(lane < TOK, t, 0.0)

    none = jnp.zeros((8, 128), F32)

    def blocks(head):
        cols = pl.ds(pl.multiple_of(head * 128, 128), 128)
        keys = stale[0, :, cols].astype(F32)
        vals = jnp.concatenate([stale[1, :, cols].astype(F32), none], axis=0).T.astype(BF16)
        x = stream[:, cols].astype(F32)
        halves = []
        for third in range(3):
            t = turned(x, third)
            halves.append(jnp.where(section == 0, t[0:64], t[TOK - 64 : TOK]).astype(BF16))
        return keys, vals, halves

    def put(at, keys, vals, x, third):
        out[at, 0:128] = jnp.concatenate([keys, aux[third]], axis=0).astype(BF16)
        out[at, 128:256] = vals
        out[at, 256:CHUNK] = x

    more_keys, more_vals, more_x = blocks(16 + step)
    for y in range(4):
        keys, vals, halves = blocks(4 * step + y)
        for third in range(3):
            put(4 * y + third, keys, vals, halves[third], third)
        put(4 * y + 3, more_keys, more_vals, more_x[y % 3], y % 3)


def pack(section, stale, stream, frames):
    grid = pltpu.PrefetchScalarGridSpec(
        num_scalar_prefetch=1,
        grid=(4,),
        in_specs=[
            pl.BlockSpec((2, TOK, WIDTH), lambda r, s: (0, 0, 0)),
            pl.BlockSpec((TOK, WIDTH), lambda r, s: (0, 0)),
            pl.BlockSpec((1, TOK), lambda r, s: (0, 0)),
        ],
        out_specs=pl.BlockSpec((16, CHUNK, 128), lambda r, s: (r, 0, 0)),
        scratch_shapes=[pltpu.VMEM((3, 8, 128), F32), pltpu.VMEM((8, 128), F32)],
    )
    return pl.pallas_call(
        pack_kernel,
        grid_spec=grid,
        out_shape=jax.ShapeDtypeStruct((64, CHUNK, 128), BF16),
        compiler_params=PARAMS,
        name="pack",
    )(section, stale, stream, frames)


def mod_table(frame_mod, with_scale):
    hi, mid, low = split3(frame_mod)
    table = jnp.concatenate([hi, mid, low, jnp.zeros((16, frame_mod.shape[1]), F32)], axis=0)
    if with_scale:
        row = lax.broadcasted_iota(jnp.int32, (64, 128), 0)
        extra = jnp.where((row >= 48) & (row < 51), 1.0, 0.0)
        table = jnp.concatenate([table, extra], axis=1)
    return table.astype(BF16)


def hot_rows(aux):
    row = lax.broadcasted_iota(jnp.int32, (48, 128), 0)
    hot = jnp.where((row & 15).astype(F32) == aux[3:4, :], 1.0, 0.0)
    return jnp.concatenate([hot, aux, jnp.zeros((8, 128), F32)], axis=0).astype(BF16)


def place_keys(p, kv, ka, vt):
    row = lax.broadcasted_iota(jnp.int32, (128, 128), 0)
    col = lax.broadcasted_iota(jnp.int32, (128, 128), 1)
    at = pl.ds(pl.multiple_of(p * 128, 128), 128)
    hidden = (col == p) | ((col == PATCHES) & (row >= TOK))
    ka[at, 0:128] = kv[0, p, 0:128, :]
    ka[at, 128:256] = jnp.where(hidden, -BIG, 0.0).astype(BF16)
    vt[0:128, at] = kv[0, p, 128:256, :]
    vt[128:144, at] = jnp.ones((16, 128), BF16)


def place_pair(t, hids, maps, qa, of, mf):
    row = lax.broadcasted_iota(jnp.int32, (80, 128), 0)
    col = lax.broadcasted_iota(jnp.int32, (80, 128), 1)
    patch = 2 * t + jnp.where(row >= THIRD, 1, 0)
    at = pl.ds(pl.multiple_of(t * 80, 16), 80)
    q = (jnp.concatenate([hid[0:THIRD] for hid in hids], axis=0) * maps[0:1, :]).astype(BF16)
    qa[at, 0:128] = q
    qa[at, 128:256] = jnp.where((col == patch) | (col == PATCHES), 1.0, 0.0).astype(BF16)
    keys = jnp.concatenate([(hid * maps[1:2, :]).astype(BF16) for hid in hids], axis=0)
    vals = jnp.concatenate([(hid * maps[2:3, :]).astype(BF16) for hid in hids], axis=0)
    s = dot(q, keys, NT)
    s = jnp.concatenate([s[0:THIRD, 0:128], s[THIRD:80, 128:256]], axis=0)
    s = jnp.where(col < TOK, s, -BIG)
    top = jnp.max(s, axis=1, keepdims=True)
    power = jnp.exp2((s - top) * FACTOR)
    none = jnp.zeros((THIRD, 128), F32)
    both = [
        jnp.concatenate([power[0:THIRD], none], axis=1),
        jnp.concatenate([none, power[THIRD:80]], axis=1),
    ]
    both = jnp.concatenate(both, axis=0).astype(BF16)
    vals = jnp.concatenate([vals, jnp.ones((256, 128), BF16)], axis=1)
    of[at, :] = dot(both, vals, NN)
    mf[at, :] = jnp.broadcast_to(top, (80, 128))


def attention(qa, ka, vt, of, mf, xo, go, sc, pt, result):
    step = 512
    begins = range(0, PATCHES * 128, step)
    tiles = OWN_ROWS // TILE
    tops = [None] * tiles

    def score(tile, begin):
        s = dot(ka[begin : begin + step, :], qa[tile * TILE : tile * TILE + TILE, :], NT)
        sc[tile % 2, begin : begin + step, :] = s
        top = jnp.max(s.reshape(step // 8, 8, TILE), axis=0)
        tops[tile] = top if begin == 0 else jnp.maximum(tops[tile], top)

    def weigh(tile, begin, top):
        s = sc[tile % 2, begin : begin + step, :]
        pt[tile % 2, begin : begin + step, :] = jnp.exp2((s - top) * FACTOR).astype(BF16)

    def finish(tile, top):
        total = dot(vt[...], pt[tile % 2], NN)
        own = total[0:128].T
        stats = jnp.concatenate([total[128:136], jnp.broadcast_to(top, (8, TILE))], axis=0).T
        at = slice(tile * TILE, tile * TILE + TILE)
        top_s, top_f = stats[:, 8:9], mf[at, 0:1]
        top = jnp.maximum(top_s, top_f)
        a, b = jnp.exp2((top_s - top) * FACTOR), jnp.exp2((top_f - top) * FACTOR)
        fresh = of[at, :]
        attended = (a * own + b * fresh[:, 0:128]) / (a * stats[:, 0:1] + b * fresh[:, 128:256])
        result(at, (xo[at, :] + go[at, :] * attended).astype(BF16))

    for begin in begins:
        score(0, begin)
    for tile in range(tiles):
        top = jnp.max(tops[tile], axis=0, keepdims=True)
        for begin in begins:
            if tile + 1 < tiles:
                score(tile + 1, begin)
            weigh(tile, begin, top)
        finish(tile, top)


def first_kernel(kv, x_rest, frame_mod, maps, x_out, sums, qa, ka, vt, of, mf, xo, go, sc, pt, sq):
    table = mod_table(frame_mod[...], True)
    gains = maps[...]

    @pl.loop(0, 4)
    def _(block):
        for sub in range(4):
            t = block * 4 + sub
            hids, xs, gates = [], [], []
            for half in range(2):
                p = 2 * t + half
                aux = kv[0, p, 112:128, :].astype(F32)[8:16]
                xa = kv[0, p, 256:CHUNK, :].astype(F32)
                xb = x_rest[0, p].astype(F32)[8:64]
                x = jnp.concatenate([xa, xb, jnp.zeros((8, 128), F32)], axis=0)
                m = dot(hot_rows(aux), table, TN)
                hid = x * m[:, 384:512] * (1.0 + m[:, 128:256]) + m[:, 0:128]
                place_keys(p, kv, ka, vt)
                hids.append(hid)
                xs.append(x[0:THIRD])
                gates.append(m[0:THIRD, 256:384])
            place_pair(t, hids, gains, qa, of, mf)
            at = pl.ds(pl.multiple_of(t * 80, 16), 80)
            xo[at, :] = jnp.concatenate(xs, axis=0)
            go[at, :] = jnp.concatenate(gates, axis=0)

    def result(at, value):
        x_out[at, :] = value
        wide = value.astype(F32)
        sq[at, :] = wide * wide

    attention(qa, ka, vt, of, mf, xo, go, sc, pt, result)
    square = sq[...]
    hi = square.astype(BF16)
    low = (square - hi.astype(F32)).astype(BF16)
    ones = jnp.ones((8, 128), BF16)
    total = dot(ones, hi, NT) + dot(ones, low, NT)
    sums[...] = total


def mid_kernel(x, total, mid):
    hi = total[...].astype(BF16).astype(F32)
    low = total[...] - hi
    rows = [part[0:1, 128 * i : 128 * i + 128] for part in (hi, low) for i in range(10)]
    sums = jnp.concatenate(rows + [jnp.zeros((4, 128), F32)], axis=0)
    for t in range(PATCHES // 2):
        pair = x[80 * t : 80 * t + 80, :].astype(F32)
        for half in range(2):
            p = 2 * t + half
            block = jnp.concatenate([pair[THIRD * half : THIRD * half + THIRD], sums], axis=0).astype(BF16)
            mid[p] = block
            mid[PATCHES + p] = block


def middle(x, total):
    whole = pl.BlockSpec(memory_space=pltpu.VMEM)
    return pl.pallas_call(
        mid_kernel,
        in_specs=[whole, whole],
        out_specs=whole,
        out_shape=jax.ShapeDtypeStruct((64, MID, 128), BF16),
        compiler_params=PARAMS,
        name="middle",
    )(x, total)


SCRATCH = [
    pltpu.VMEM((OWN_ROWS, 256), BF16),
    pltpu.VMEM((PATCHES * 128, 256), BF16),
    pltpu.VMEM((144, PATCHES * 128), BF16),
    pltpu.VMEM((OWN_ROWS, 256), F32),
    pltpu.VMEM((OWN_ROWS, 128), F32),
    pltpu.VMEM((OWN_ROWS, 128), F32),
    pltpu.VMEM((OWN_ROWS, 128), F32),
    pltpu.VMEM((2, PATCHES * 128, TILE), F32),
    pltpu.VMEM((2, PATCHES * 128, TILE), BF16),
]


def first_layer(received, frame_mod, maps):
    return pl.pallas_call(
        first_kernel,
        grid=(1,),
        in_specs=[
            pl.BlockSpec((1, PATCHES, CHUNK, 128), lambda i: (0, 0, 0, 0)),
            pl.BlockSpec((1, PATCHES, 64, 128), lambda i: (1, 0, 4, 0)),
            pl.BlockSpec((16, 384), lambda i: (0, 0)),
            pl.BlockSpec((3, 128), lambda i: (0, 0)),
        ],
        out_specs=[
            pl.BlockSpec((OWN_ROWS, 128), lambda i: (0, 0)),
            pl.BlockSpec((8, OWN_ROWS), lambda i: (0, 0)),
        ],
        out_shape=[
            jax.ShapeDtypeStruct((OWN_ROWS, 128), BF16),
            jax.ShapeDtypeStruct((8, OWN_ROWS), F32),
        ],
        scratch_shapes=SCRATCH + [pltpu.VMEM((OWN_ROWS, 128), F32)],
        compiler_params=PARAMS,
        name="first_layer",
    )(received, received, frame_mod, maps)


def second_kernel(scal, kv, own, after, before, sums, frame_mod, maps, x_out, qa, ka, vt, of, mf, xo, go, sc, pt, rs):
    table = mod_table(frame_mod[...], False)
    gains = maps[...]
    third = scal[0]
    row = lax.broadcasted_iota(jnp.int32, (16, OWN_ROWS), 0)
    ones = jnp.where(lax.broadcasted_iota(jnp.int32, (16, 128), 0) < 3, 1.0, 0.0).astype(BF16)
    for k in range(3):
        which = lax.rem(third + k, 3)
        total = None
        for head in range(HEADS):
            at = 4 * head + which if head < 16 else 16 * (head - 16) + 4 * which + 3
            part = sums[at].astype(F32)
            total = part if total is None else total + part
        square = jnp.concatenate([total[8 + i : 9 + i] + total[18 + i : 19 + i] for i in range(10)], axis=1)
        hi, mid, low = split3(lax.rsqrt(square * (1.0 / WIDTH) + EPSILON))
        r = jnp.where(row == 0, hi, jnp.where(row == 1, mid, jnp.where(row == 2, low, 0.0)))
        rs[k] = dot(r.astype(BF16), ones, TN)

    @pl.loop(0, 4)
    def _(block):
        for sub in range(4):
            t = block * 4 + sub
            at = pl.ds(pl.multiple_of(t * 80, 16), 80)
            pair = [ref[at, :].astype(F32) for ref in (own, after, before)]
            scale = [rs[k, at, :] for k in range(3)]
            hids, gates = [], []
            for half in range(2):
                p = 2 * t + half
                cut = slice(THIRD * half, THIRD * half + THIRD)
                aux = kv[0, p, 112:128, :].astype(F32)[8:16]
                none = [jnp.zeros((8, 128), F32)]
                x = jnp.concatenate([v[cut] for v in pair] + none, axis=0)
                r = jnp.concatenate([v[cut] for v in scale] + none, axis=0)
                m = dot(hot_rows(aux), table, TN)
                hid = x * r * (1.0 + m[:, 128:256]) + m[:, 0:128]
                place_keys(p, kv, ka, vt)
                hids.append(hid)
                gates.append(m[0:THIRD, 256:384])
            place_pair(t, hids, gains, qa, of, mf)
            xo[at, :] = pair[0]
            go[at, :] = jnp.concatenate(gates, axis=0)

    def result(at, value):
        x_out[at, :] = value

    attention(qa, ka, vt, of, mf, xo, go, sc, pt, result)


def second_layer(third, received, own, after, before, sums, frame_mod, maps):
    rows = pl.BlockSpec((OWN_ROWS, 128), lambda i, s: (0, 0))
    grid = pltpu.PrefetchScalarGridSpec(
        num_scalar_prefetch=1,
        grid=(1,),
        in_specs=[
            pl.BlockSpec((1, PATCHES, 256, 128), lambda i, s: (1, 0, 0, 0)),
            rows,
            rows,
            rows,
            pl.BlockSpec((64, 32, 128), lambda i, s: (0, 1, 0)),
            pl.BlockSpec((16, 384), lambda i, s: (0, 0)),
            pl.BlockSpec((3, 128), lambda i, s: (0, 0)),
        ],
        out_specs=rows,
        scratch_shapes=SCRATCH + [pltpu.VMEM((3, OWN_ROWS, 128), F32)],
    )
    return pl.pallas_call(
        second_kernel,
        grid_spec=grid,
        out_shape=jax.ShapeDtypeStruct((OWN_ROWS, 128), BF16),
        compiler_params=PARAMS,
        name="second_layer",
    )(third, received, own, after, before, sums, frame_mod, maps)


def home_kernel(scal, got, stream, frames, frame_mod, maps, out, xs, frame_row):
    section = scal[0]
    frame_row[0:1, 0:TOK] = frames[...].astype(F32)
    square = jnp.zeros((TOK, 128), F32)
    for head in range(HEADS):
        cols = slice(128 * head, 128 * head + 128)
        parts = [got[place_of(head, third)].astype(F32)[0:THIRD] for third in range(3)]
        x = jnp.where(section == 0, stream[:, cols].astype(F32), jnp.concatenate(parts, axis=0))
        xs[:, cols] = x
        square = square + x * x
    r = lax.rsqrt(jnp.sum(square, axis=1, keepdims=True) * (1.0 / WIDTH) + EPSILON)
    row = lax.broadcasted_iota(jnp.int32, (48, 128), 0)
    hot = jnp.where((row & 15).astype(F32) == frame_row[0:1, :], 1.0, 0.0).astype(BF16)
    for head in range(HEADS):
        cols = slice(128 * head, 128 * head + 128)
        more = slice(WIDTH + 128 * head, WIDTH + 128 * head + 128)
        mod = jnp.concatenate([frame_mod[:, cols], frame_mod[:, more]], axis=1)
        m = dot(hot, jnp.concatenate(split3(mod), axis=0).astype(BF16), TN)[0:TOK]
        hid = xs[:, cols] * r * (1.0 + m[:, 128:256]) + m[:, 0:128]
        out[0, :, cols] = (hid * maps[1:2, cols]).astype(BF16)
        out[1, :, cols] = (hid * maps[2:3, cols]).astype(BF16)


def home(section, got, stream, frames, frame_mod, maps):
    whole = pl.BlockSpec(memory_space=pltpu.VMEM)
    return pl.pallas_call(
        home_kernel,
        in_specs=[pl.BlockSpec(memory_space=pltpu.SMEM)] + [whole] * 5,
        out_specs=whole,
        out_shape=jax.ShapeDtypeStruct((2, TOK, WIDTH), BF16),
        scratch_shapes=[pltpu.VMEM((TOK, WIDTH), F32), pltpu.VMEM((8, 128), F32)],
        compiler_params=PARAMS,
        name="home",
    )(section, got, stream, frames, frame_mod, maps)


def unpack_kernel(scal, got, out):
    branch = scal[0]
    for j in range(HEADS // 2):
        parts = []
        for third in range(3):
            a, b = place_of(j, third), place_of(j + HEADS // 2, third)
            parts.append(got[jnp.where(branch == 0, a, b)].astype(F32))
        out[:, 128 * j : 128 * j + 128] = jnp.concatenate(parts, axis=0).astype(BF16)


def unpack(branch, got):
    whole = pl.BlockSpec(memory_space=pltpu.VMEM)
    return pl.pallas_call(
        unpack_kernel,
        in_specs=[pl.BlockSpec(memory_space=pltpu.SMEM), whole],
        out_specs=whole,
        out_shape=jax.ShapeDtypeStruct((TOK, WIDTH // 2), BF16),
        compiler_params=PARAMS,
        name="unpack",
    )(branch, got)


def body(stream, token_frame, frame_levels, level_table, branch_mod, layer_mod, maps, stale_kv):
    section = lax.axis_index("section")
    branch = lax.axis_index("branch")
    place = section * PATCHES + lax.axis_index("patch")
    x, y, z = place % 4, (place // 4) % 4, place // 16
    head = jnp.where(x < 3, place // 4, 16 + z)
    third = jnp.where(x < 3, x, jnp.where(y < 3, y, 0))

    both = jnp.concatenate([layer_mod.reshape(3, WIDTH), maps[0]], axis=0)
    other = lax.ppermute(both, "section", [(0, 1), (1, 0)])

    frames = token_frame.reshape(1, TOK)
    section_at = section.reshape(1).astype(jnp.int32)
    send = pack(section_at, stale_kv[0, 0], stream, frames)
    received = lax.all_to_all(send, PLANE, 0, 0, tiled=True)
    received = received.reshape(2, PATCHES, CHUNK, 128)

    level_hot = (frame_levels[:, None] == jnp.arange(LEVELS, dtype=jnp.int32)[None, :]).astype(F32)
    base = jnp.dot(level_hot, level_table, precision=lax.Precision.HIGHEST, preferred_element_type=F32)
    home_mod = base + (layer_mod[0] + branch_mod[0])[None, :]

    def of_head(array):
        rows = array.shape[0]
        return lax.dynamic_slice_in_dim(array.reshape(rows, -1, HEADS, 128), head, 1, 2)[:, :, 0]

    layers = jnp.stack([jnp.where(section == 0, both, other), jnp.where(section == 0, other, both)])
    mine = of_head(layers.reshape(12, WIDTH)).reshape(2, 6, 128)
    base_mine = of_head(base)
    branch_mine = of_head(branch_mod)[0]
    mods = base_mine[None] + (mine[:, 0:3] + branch_mine[None])[:, None]
    mods = mods.reshape(2, FRAMES, 384)
    gains = mine[:, 3:6]

    x_one, total = first_layer(received, mods[0], gains[0])

    def from_third(by):
        pairs = [(place_of(h, (g + by) % 3), place_of(h, g)) for h in range(HEADS) for g in range(3)]
        return lax.ppermute(x_one, PLANE, pairs)

    after, before = from_third(1), from_third(2)
    mid = middle(x_one, total)
    mid_got = lax.all_to_all(mid, PLANE, 0, 0, tiled=True)
    fresh = home(section_at, mid_got, stream, frames, home_mod, maps[0])
    x_two = second_layer(third.reshape(1).astype(jnp.int32), received, x_one, after, before, mid_got, mods[1], gains[1])

    x_other = lax.ppermute(x_two, "branch", [(0, 1), (1, 0)])
    cond = jnp.where(branch == 0, x_two, x_other).astype(F32)
    uncond = jnp.where(branch == 0, x_other, x_two).astype(F32)
    guided = (uncond + GUIDE * (cond - uncond)).astype(BF16).reshape(1, PATCHES, THIRD, 128)
    guided = jnp.broadcast_to(guided, (2, PATCHES, THIRD, 128)).reshape(64, THIRD, 128)
    guided_got = lax.all_to_all(guided, PLANE, 0, 0, tiled=True)
    out = unpack(branch.reshape(1).astype(jnp.int32), guided_got)
    return (out, fresh[None, None])


def solution(mesh):
    placed = (
        P("patch", None),
        P("patch"),
        P(),
        P(),
        P("branch", None),
        P("section", None),
        P("section", None, None),
        P("branch", "section", None, "patch", None),
    )
    return jax.shard_map(
        body,
        mesh=mesh,
        in_specs=placed,
        out_specs=(P("patch", "branch"), P("branch", "section", None, "patch", None)),
        check_vma=False,
    )
```

```python
import functools
import math

import jax
import jax.numpy as jnp
from jax import lax
from jax.experimental import pallas as pl
from jax.experimental.pallas import tpu as pltpu
from jax.sharding import PartitionSpec as P

HEADS = 20
HEAD_DIM = 128
FRAMES = 16
LEVELS = 50
TOK = 120
THIRD = 40
PATCHES = 32
WIDTH = HEADS * HEAD_DIM
EPSILON = 1e-06
GUIDE = 5.0
BIG = 1e30
PLANE = ("section", "patch")
F32 = jnp.float32
BF16 = jnp.bfloat16
VMEM_BYTES = 56 * 1024 * 1024
PARAMS = pltpu.CompilerParams(vmem_limit_bytes=VMEM_BYTES)

OWN_ROWS = PATCHES * THIRD
TILE = 640
FACTOR = HEAD_DIM ** (-0.5) * math.log2(math.e)
CHUNK = 320
MID = 64


def place_of(head, third):
    if head < 16:
        return 4 * head + third
    return 16 * (head - 16) + 4 * third + 3


def dot(a, b, dims):
    return lax.dot_general(a, b, (dims, ((), ())), preferred_element_type=F32)


NN = ((1,), (0,))
NT = ((1,), (1,))
TN = ((0,), (0,))


def split3(v):
    hi = v.astype(BF16).astype(F32)
    mid = (v - hi).astype(BF16).astype(F32)
    low = (v - hi - mid).astype(BF16).astype(F32)
    return hi, mid, low


def turned(rows, third):
    cut = THIRD * third
    return rows if cut == 0 else jnp.concatenate([rows[cut:TOK], rows[:cut]], axis=0)


def pack_kernel(scal, stale, stream, frames, out, aux, frame_row):
    step = pl.program_id(0)
    section = scal[0]

    @pl.when(step == 0)
    def _():
        frame_row[...] = jnp.zeros((8, 128), F32)
        frame_row[0:1, 0:TOK] = frames[...].astype(F32)
        square = jnp.zeros((TOK, 128), F32)
        for head in range(HEADS):
            part = stream[:, 128 * head : 128 * head + 128].astype(F32)
            square = square + part * part
        square = jnp.concatenate([square, jnp.zeros((8, 128), F32)], axis=0)
        total = jnp.sum(square.T, axis=0, keepdims=True)
        r = lax.rsqrt(total * (1.0 / WIDTH) + EPSILON)
        hi, mid, low = split3(jnp.broadcast_to(r, (8, 128)))
        row = lax.broadcasted_iota(jnp.int32, (8, 128), 0)
        lane = lax.broadcasted_iota(jnp.int32, (8, 128), 1)
        a = jnp.where(row == 0, hi, jnp.where(row == 1, mid, jnp.where(row == 2, low, 0.0)))
        a = jnp.where(row == 3, frame_row[0:1, :], a)
        a = jnp.where(lane < TOK, a, 0.0)
        aux[0] = a
        for third in range(1, 3):
            cut = THIRD * third
            t = jnp.where(lane < TOK - cut, pltpu.roll(a, 128 - cut, 1), pltpu.roll(a, TOK - cut, 1))
            aux[third] = jnp.where(lane < TOK, t, 0.0)

    none = jnp.zeros((8, 128), F32)

    def blocks(head):
        cols = pl.ds(pl.multiple_of(head * 128, 128), 128)
        keys = stale[0, :, cols].astype(F32)
        vals = jnp.concatenate([stale[1, :, cols].astype(F32), none], axis=0).T.astype(BF16)
        x = stream[:, cols].astype(F32)
        halves = []
        for third in range(3):
            t = turned(x, third)
            halves.append(jnp.where(section == 0, t[0:64], t[TOK - 64 : TOK]).astype(BF16))
        return keys, vals, halves

    def put(at, keys, vals, x, third):
        out[at, 0:128] = jnp.concatenate([keys, aux[third]], axis=0).astype(BF16)
        out[at, 128:256] = vals
        out[at, 256:CHUNK] = x

    more_keys, more_vals, more_x = blocks(16 + step)
    for y in range(4):
        keys, vals, halves = blocks(4 * step + y)
        for third in range(3):
            put(4 * y + third, keys, vals, halves[third], third)
        put(4 * y + 3, more_keys, more_vals, more_x[y % 3], y % 3)


def pack(section, stale, stream, frames):
    grid = pltpu.PrefetchScalarGridSpec(
        num_scalar_prefetch=1,
        grid=(4,),
        in_specs=[
            pl.BlockSpec((2, TOK, WIDTH), lambda r, s: (0, 0, 0)),
            pl.BlockSpec((TOK, WIDTH), lambda r, s: (0, 0)),
            pl.BlockSpec((1, TOK), lambda r, s: (0, 0)),
        ],
        out_specs=pl.BlockSpec((16, CHUNK, 128), lambda r, s: (r, 0, 0)),
        scratch_shapes=[pltpu.VMEM((3, 8, 128), F32), pltpu.VMEM((8, 128), F32)],
    )
    return pl.pallas_call(
        pack_kernel,
        grid_spec=grid,
        out_shape=jax.ShapeDtypeStruct((64, CHUNK, 128), BF16),
        compiler_params=PARAMS,
        name="pack",
    )(section, stale, stream, frames)


def mod_table(frame_mod, with_scale):
    hi, mid, low = split3(frame_mod)
    table = jnp.concatenate([hi, mid, low, jnp.zeros((16, frame_mod.shape[1]), F32)], axis=0)
    if with_scale:
        row = lax.broadcasted_iota(jnp.int32, (64, 128), 0)
        extra = jnp.where((row >= 48) & (row < 51), 1.0, 0.0)
        table = jnp.concatenate([table, extra], axis=1)
    return table.astype(BF16)


def hot_rows(aux):
    row = lax.broadcasted_iota(jnp.int32, (48, 128), 0)
    hot = jnp.where((row & 15).astype(F32) == aux[3:4, :], 1.0, 0.0)
    return jnp.concatenate([hot, aux, jnp.zeros((8, 128), F32)], axis=0).astype(BF16)


def modulations(kv, table, mods):
    for begin in range(0, PATCHES, 8):
        hot = [hot_rows(kv[0, p, 112:128, :].astype(F32)[8:16]) for p in range(begin, begin + 8)]
        at = slice(begin * 128, begin * 128 + 1024)
        mods[at, 0 : table.shape[1]] = dot(jnp.concatenate(hot, axis=1), table, TN)


def place_pair(t, hids, maps, kv, qa, ka, vt, kf, vh):
    row = lax.broadcasted_iota(jnp.int32, (80, 128), 0)
    col = lax.broadcasted_iota(jnp.int32, (80, 128), 1)
    patch = 2 * t + jnp.where(row >= THIRD, 1, 0)
    at = slice(t * 80, t * 80 + 80)
    q = jnp.concatenate([hid[0:THIRD] for hid in hids], axis=0) * maps[0:1, :]
    qa[at, 0:128] = q.astype(BF16)
    qa[at, 128:256] = jnp.where((col == patch) | (col == PATCHES), 1.0, 0.0).astype(BF16)
    row = lax.broadcasted_iota(jnp.int32, (128, 128), 0)
    col = lax.broadcasted_iota(jnp.int32, (128, 128), 1)
    for half in range(2):
        p = 2 * t + half
        at = slice(p * 128, p * 128 + 128)
        ka[at, 0:128] = kv[0, p, 0:128, :]
        hidden = (col == p) | ((col == PATCHES) & (row >= TOK))
        ka[at, 128:256] = jnp.where(hidden, -BIG, 0.0).astype(BF16)
        vt[0:128, at] = kv[0, p, 128:256, :]
        kf[at, 0:128] = (hids[half] * maps[1:2, :]).astype(BF16)
        hidden = (col <= PATCHES) & ((row >= TOK) | ((col != p) & (col < PATCHES)))
        kf[at, 128:256] = jnp.where(hidden, -BIG, 0.0).astype(BF16)
        vh[at, :] = (hids[half] * maps[2:3, :]).astype(BF16)


def turn_values(vh, vt, vf):
    row = lax.broadcasted_iota(jnp.int32, (128, 128), 0)
    col = lax.broadcasted_iota(jnp.int32, (128, 128), 1)
    unit = jnp.where(row == col, 1.0, 0.0).astype(BF16)
    for begin in range(0, PATCHES * 128, 1024):
        at = slice(begin, begin + 1024)
        vf[0:128, at] = dot(unit, vh[at, :], NT).astype(BF16)
    vt[128:144, :] = jnp.ones((16, PATCHES * 128), BF16)
    vf[128:144, :] = jnp.ones((16, PATCHES * 128), BF16)


def attention(qa, ka, vt, kf, vf, xo, go, sc, pt, result):
    step = 512
    stale = PATCHES * 128
    begins = range(0, stale + step, step)
    row = lax.broadcasted_iota(jnp.int32, (128, 256), 0)
    col = lax.broadcasted_iota(jnp.int32, (128, 256), 1)
    unit = jnp.where((row == col) | (row + 128 == col), 1.0, 0.0).astype(BF16)

    def fresh_at(tile, j):
        low = (tile * (TILE // THIRD) + 3 * j) * 128
        return slice(low, low + step)

    for tile in range(OWN_ROWS // TILE):
        first = tile * TILE
        top = None
        for begin in begins:
            if begin < stale:
                s = dot(ka[begin : begin + step, :], qa[first : first + TILE, :], NT)
            else:
                parts = [
                    dot(kf[fresh_at(tile, j), :], qa[first + 128 * j : first + 128 * j + 128, :], NT)
                    for j in range(TILE // 128)
                ]
                s = jnp.concatenate(parts, axis=1)
            sc[begin : begin + step, :] = s
            here = jnp.max(s.reshape(step // 8, 8, TILE), axis=0)
            top = here if top is None else jnp.maximum(top, here)
        top = jnp.max(top, axis=0, keepdims=True)
        for begin in begins:
            pt[begin : begin + step, :] = jnp.exp2((sc[begin : begin + step, :] - top) * FACTOR).astype(BF16)
        total = dot(vt[...], pt[0:stale, :], NN)
        more = [
            dot(vf[:, fresh_at(tile, j)], pt[stale : stale + step, 128 * j : 128 * j + 128], NN)
            for j in range(TILE // 128)
        ]
        total = total + jnp.concatenate(more, axis=1)
        mean = total[0:128] / total[128:129]
        hi = mean.astype(BF16)
        low = (mean - hi.astype(F32)).astype(BF16)
        for j in range(TILE // 128):
            cols = slice(128 * j, 128 * j + 128)
            attended = dot(unit, jnp.concatenate([hi[:, cols], low[:, cols]], axis=1), NT)
            at = slice(first + 128 * j, first + 128 * j + 128)
            result(at, (xo[at, :] + go[at, :] * attended).astype(BF16))


def first_kernel(kv, x_rest, frame_mod, maps, x_out, sums, qa, ka, vt, kf, vf, xo, go, sc, pt, mods, vh, sq):
    table = mod_table(frame_mod[...], True)
    gains = maps[...]

    modulations(kv, table, mods)
    for t in range(PATCHES // 2):
        at = slice(t * 80, t * 80 + 80)
        hids, xs, gates = [], [], []
        for half in range(2):
            p = 2 * t + half
            xa = kv[0, p, 256:CHUNK, :].astype(F32)
            xb = x_rest[0, p].astype(F32)[8:64]
            x = jnp.concatenate([xa, xb, jnp.zeros((8, 128), F32)], axis=0)
            m = mods[p * 128 : p * 128 + 128, :]
            hids.append(x * m[:, 384:512] * (1.0 + m[:, 128:256]) + m[:, 0:128])
            xs.append(x[0:THIRD])
            gates.append(m[0:THIRD, 256:384])
        place_pair(t, hids, gains, kv, qa, ka, vt, kf, vh)
        xo[at, :] = jnp.concatenate(xs, axis=0)
        go[at, :] = jnp.concatenate(gates, axis=0)
    turn_values(vh, vt, vf)

    def result(at, value):
        x_out[at, :] = value
        wide = value.astype(F32)
        sq[at, :] = wide * wide

    attention(qa, ka, vt, kf, vf, xo, go, sc, pt, result)
    square = sq[...]
    hi = square.astype(BF16)
    low = (square - hi.astype(F32)).astype(BF16)
    ones = jnp.ones((8, 128), BF16)
    total = dot(ones, hi, NT) + dot(ones, low, NT)
    sums[...] = total


def mid_kernel(x, total, mid):
    hi = total[...].astype(BF16).astype(F32)
    low = total[...] - hi
    rows = [part[0:1, 128 * i : 128 * i + 128] for part in (hi, low) for i in range(10)]
    sums = jnp.concatenate(rows + [jnp.zeros((4, 128), F32)], axis=0)
    for t in range(PATCHES // 2):
        pair = x[80 * t : 80 * t + 80, :].astype(F32)
        for half in range(2):
            p = 2 * t + half
            block = jnp.concatenate([pair[THIRD * half : THIRD * half + THIRD], sums], axis=0).astype(BF16)
            mid[p] = block
            mid[PATCHES + p] = block


def middle(x, total):
    whole = pl.BlockSpec(memory_space=pltpu.VMEM)
    return pl.pallas_call(
        mid_kernel,
        in_specs=[whole, whole],
        out_specs=whole,
        out_shape=jax.ShapeDtypeStruct((64, MID, 128), BF16),
        compiler_params=PARAMS,
        name="middle",
    )(x, total)


SCRATCH = [
    pltpu.VMEM((OWN_ROWS, 256), BF16),
    pltpu.VMEM((PATCHES * 128, 256), BF16),
    pltpu.VMEM((144, PATCHES * 128), BF16),
    pltpu.VMEM((PATCHES * 128, 256), BF16),
    pltpu.VMEM((144, PATCHES * 128), BF16),
    pltpu.VMEM((OWN_ROWS, 128), F32),
    pltpu.VMEM((OWN_ROWS, 128), F32),
    pltpu.VMEM((PATCHES * 128 + 512, TILE), F32),
    pltpu.VMEM((PATCHES * 128 + 512, TILE), BF16),
    pltpu.VMEM((PATCHES * 128, 512), F32),
    pltpu.VMEM((PATCHES * 128, 128), BF16),
]


def first_layer(received, frame_mod, maps):
    return pl.pallas_call(
        first_kernel,
        grid=(1,),
        in_specs=[
            pl.BlockSpec((1, PATCHES, CHUNK, 128), lambda i: (0, 0, 0, 0)),
            pl.BlockSpec((1, PATCHES, 64, 128), lambda i: (1, 0, 4, 0)),
            pl.BlockSpec((16, 384), lambda i: (0, 0)),
            pl.BlockSpec((3, 128), lambda i: (0, 0)),
        ],
        out_specs=[
            pl.BlockSpec((OWN_ROWS, 128), lambda i: (0, 0)),
            pl.BlockSpec((8, OWN_ROWS), lambda i: (0, 0)),
        ],
        out_shape=[
            jax.ShapeDtypeStruct((OWN_ROWS, 128), BF16),
            jax.ShapeDtypeStruct((8, OWN_ROWS), F32),
        ],
        scratch_shapes=SCRATCH + [pltpu.VMEM((OWN_ROWS, 128), F32)],
        compiler_params=PARAMS,
        name="first_layer",
    )(received, received, frame_mod, maps)


def second_kernel(scal, kv, own, after, before, sums, frame_mod, maps, x_out, qa, ka, vt, kf, vf, xo, go, sc, pt, mods, vh, rs):
    table = mod_table(frame_mod[...], False)
    gains = maps[...]
    third = scal[0]
    row = lax.broadcasted_iota(jnp.int32, (16, OWN_ROWS), 0)
    ones = jnp.where(lax.broadcasted_iota(jnp.int32, (16, 128), 0) < 3, 1.0, 0.0).astype(BF16)
    for k in range(3):
        which = lax.rem(third + k, 3)
        total = None
        for head in range(HEADS):
            at = 4 * head + which if head < 16 else 16 * (head - 16) + 4 * which + 3
            part = sums[at].astype(F32)
            total = part if total is None else total + part
        square = jnp.concatenate([total[8 + i : 9 + i] + total[18 + i : 19 + i] for i in range(10)], axis=1)
        hi, mid, low = split3(lax.rsqrt(square * (1.0 / WIDTH) + EPSILON))
        r = jnp.where(row == 0, hi, jnp.where(row == 1, mid, jnp.where(row == 2, low, 0.0)))
        rs[k] = dot(r.astype(BF16), ones, TN)

    modulations(kv, table, mods)
    for t in range(PATCHES // 2):
        at = slice(t * 80, t * 80 + 80)
        pair = [ref[at, :].astype(F32) for ref in (own, after, before)]
        scale = [rs[k, at, :] for k in range(3)]
        hids, gates = [], []
        for half in range(2):
            p = 2 * t + half
            cut = slice(THIRD * half, THIRD * half + THIRD)
            none = [jnp.zeros((8, 128), F32)]
            x = jnp.concatenate([v[cut] for v in pair] + none, axis=0)
            r = jnp.concatenate([v[cut] for v in scale] + none, axis=0)
            m = mods[p * 128 : p * 128 + 128, 0:384]
            hids.append(x * r * (1.0 + m[:, 128:256]) + m[:, 0:128])
            gates.append(m[0:THIRD, 256:384])
        place_pair(t, hids, gains, kv, qa, ka, vt, kf, vh)
        xo[at, :] = pair[0]
        go[at, :] = jnp.concatenate(gates, axis=0)
    turn_values(vh, vt, vf)

    def result(at, value):
        x_out[at, :] = value

    attention(qa, ka, vt, kf, vf, xo, go, sc, pt, result)


def second_layer(third, received, own, after, before, sums, frame_mod, maps):
    rows = pl.BlockSpec((OWN_ROWS, 128), lambda i, s: (0, 0))
    grid = pltpu.PrefetchScalarGridSpec(
        num_scalar_prefetch=1,
        grid=(1,),
        in_specs=[
            pl.BlockSpec((1, PATCHES, 256, 128), lambda i, s: (1, 0, 0, 0)),
            rows,
            rows,
            rows,
            pl.BlockSpec((64, 32, 128), lambda i, s: (0, 1, 0)),
            pl.BlockSpec((16, 384), lambda i, s: (0, 0)),
            pl.BlockSpec((3, 128), lambda i, s: (0, 0)),
        ],
        out_specs=rows,
        scratch_shapes=SCRATCH + [pltpu.VMEM((3, OWN_ROWS, 128), F32)],
    )
    return pl.pallas_call(
        second_kernel,
        grid_spec=grid,
        out_shape=jax.ShapeDtypeStruct((OWN_ROWS, 128), BF16),
        compiler_params=PARAMS,
        name="second_layer",
    )(third, received, own, after, before, sums, frame_mod, maps)


def home_kernel(scal, got, stream, frames, frame_mod, maps, out, xs, frame_row):
    section = scal[0]
    frame_row[0:1, 0:TOK] = frames[...].astype(F32)
    square = jnp.zeros((TOK, 128), F32)
    for head in range(HEADS):
        cols = slice(128 * head, 128 * head + 128)
        parts = [got[place_of(head, third)].astype(F32)[0:THIRD] for third in range(3)]
        x = jnp.where(section == 0, stream[:, cols].astype(F32), jnp.concatenate(parts, axis=0))
        xs[:, cols] = x
        square = square + x * x
    r = lax.rsqrt(jnp.sum(square, axis=1, keepdims=True) * (1.0 / WIDTH) + EPSILON)
    row = lax.broadcasted_iota(jnp.int32, (48, 128), 0)
    hot = jnp.where((row & 15).astype(F32) == frame_row[0:1, :], 1.0, 0.0).astype(BF16)
    for head in range(HEADS):
        cols = slice(128 * head, 128 * head + 128)
        more = slice(WIDTH + 128 * head, WIDTH + 128 * head + 128)
        mod = jnp.concatenate([frame_mod[:, cols], frame_mod[:, more]], axis=1)
        m = dot(hot, jnp.concatenate(split3(mod), axis=0).astype(BF16), TN)[0:TOK]
        hid = xs[:, cols] * r * (1.0 + m[:, 128:256]) + m[:, 0:128]
        out[0, :, cols] = (hid * maps[1:2, cols]).astype(BF16)
        out[1, :, cols] = (hid * maps[2:3, cols]).astype(BF16)


def home(section, got, stream, frames, frame_mod, maps):
    whole = pl.BlockSpec(memory_space=pltpu.VMEM)
    return pl.pallas_call(
        home_kernel,
        in_specs=[pl.BlockSpec(memory_space=pltpu.SMEM)] + [whole] * 5,
        out_specs=whole,
        out_shape=jax.ShapeDtypeStruct((2, TOK, WIDTH), BF16),
        scratch_shapes=[pltpu.VMEM((TOK, WIDTH), F32), pltpu.VMEM((8, 128), F32)],
        compiler_params=PARAMS,
        name="home",
    )(section, got, stream, frames, frame_mod, maps)


def unpack_kernel(scal, got, out):
    branch = scal[0]
    for j in range(HEADS // 2):
        parts = []
        for third in range(3):
            a, b = place_of(j, third), place_of(j + HEADS // 2, third)
            parts.append(got[jnp.where(branch == 0, a, b)].astype(F32))
        out[:, 128 * j : 128 * j + 128] = jnp.concatenate(parts, axis=0).astype(BF16)


def unpack(branch, got):
    whole = pl.BlockSpec(memory_space=pltpu.VMEM)
    return pl.pallas_call(
        unpack_kernel,
        in_specs=[pl.BlockSpec(memory_space=pltpu.SMEM), whole],
        out_specs=whole,
        out_shape=jax.ShapeDtypeStruct((TOK, WIDTH // 2), BF16),
        compiler_params=PARAMS,
        name="unpack",
    )(branch, got)


def body(stream, token_frame, frame_levels, level_table, branch_mod, layer_mod, maps, stale_kv):
    section = lax.axis_index("section")
    branch = lax.axis_index("branch")
    place = section * PATCHES + lax.axis_index("patch")
    x, y, z = place % 4, (place // 4) % 4, place // 16
    head = jnp.where(x < 3, place // 4, 16 + z)
    third = jnp.where(x < 3, x, jnp.where(y < 3, y, 0))

    both = jnp.concatenate([layer_mod.reshape(3, WIDTH), maps[0]], axis=0)
    other = lax.ppermute(both, "section", [(0, 1), (1, 0)])

    frames = token_frame.reshape(1, TOK)
    section_at = section.reshape(1).astype(jnp.int32)
    send = pack(section_at, stale_kv[0, 0], stream, frames)
    received = lax.all_to_all(send, PLANE, 0, 0, tiled=True)
    received = received.reshape(2, PATCHES, CHUNK, 128)

    level_hot = (frame_levels[:, None] == jnp.arange(LEVELS, dtype=jnp.int32)[None, :]).astype(F32)
    base = jnp.dot(level_hot, level_table, precision=lax.Precision.HIGHEST, preferred_element_type=F32)
    home_mod = base + (layer_mod[0] + branch_mod[0])[None, :]

    def of_head(array):
        rows = array.shape[0]
        return lax.dynamic_slice_in_dim(array.reshape(rows, -1, HEADS, 128), head, 1, 2)[:, :, 0]

    layers = jnp.stack([jnp.where(section == 0, both, other), jnp.where(section == 0, other, both)])
    mine = of_head(layers.reshape(12, WIDTH)).reshape(2, 6, 128)
    base_mine = of_head(base)
    branch_mine = of_head(branch_mod)[0]
    mods = base_mine[None] + (mine[:, 0:3] + branch_mine[None])[:, None]
    mods = mods.reshape(2, FRAMES, 384)
    gains = mine[:, 3:6]

    x_one, total = first_layer(received, mods[0], gains[0])

    def from_third(by):
        pairs = [(place_of(h, (g + by) % 3), place_of(h, g)) for h in range(HEADS) for g in range(3)]
        return lax.ppermute(x_one, PLANE, pairs)

    after, before = from_third(1), from_third(2)
    mid = middle(x_one, total)
    mid_got = lax.all_to_all(mid, PLANE, 0, 0, tiled=True)
    fresh = home(section_at, mid_got, stream, frames, home_mod, maps[0])
    x_two = second_layer(third.reshape(1).astype(jnp.int32), received, x_one, after, before, mid_got, mods[1], gains[1])

    x_other = lax.ppermute(x_two, "branch", [(0, 1), (1, 0)])
    cond = jnp.where(branch == 0, x_two, x_other).astype(F32)
    uncond = jnp.where(branch == 0, x_other, x_two).astype(F32)
    guided = (uncond + GUIDE * (cond - uncond)).astype(BF16).reshape(1, PATCHES, THIRD, 128)
    guided = jnp.broadcast_to(guided, (2, PATCHES, THIRD, 128)).reshape(64, THIRD, 128)
    guided_got = lax.all_to_all(guided, PLANE, 0, 0, tiled=True)
    out = unpack(branch.reshape(1).astype(jnp.int32), guided_got)
    return (out, fresh[None, None])


def solution(mesh):
    placed = (
        P("patch", None),
        P("patch"),
        P(),
        P(),
        P("branch", None),
        P("section", None),
        P("section", None, None),
        P("branch", "section", None, "patch", None),
    )
    return jax.shard_map(
        body,
        mesh=mesh,
        in_specs=placed,
        out_specs=(P("patch", "branch"), P("branch", "section", None, "patch", None)),
        check_vma=False,
    )
```

```python
import functools
import math

import jax
import jax.numpy as jnp
from jax import lax
from jax.experimental import pallas as pl
from jax.experimental.pallas import tpu as pltpu
from jax.sharding import PartitionSpec as P

HEADS = 20
HEAD_DIM = 128
FRAMES = 16
LEVELS = 50
TOK = 120
THIRD = 40
PATCHES = 32
WIDTH = HEADS * HEAD_DIM
EPSILON = 1e-06
GUIDE = 5.0
BIG = 1e30
PLANE = ("section", "patch")
F32 = jnp.float32
BF16 = jnp.bfloat16
VMEM_BYTES = 56 * 1024 * 1024
PARAMS = pltpu.CompilerParams(vmem_limit_bytes=VMEM_BYTES)

OWN_ROWS = PATCHES * THIRD
TILE = 640
WIDE = 1280
SMALL = 1e-25
FACTOR = HEAD_DIM ** (-0.5) * math.log2(math.e)
CHUNK = 320
MID = 64


def place_of(head, third):
    if head < 16:
        return 4 * head + third
    return 16 * (head - 16) + 4 * third + 3


def dot(a, b, dims):
    return lax.dot_general(a, b, (dims, ((), ())), preferred_element_type=F32)


NN = ((1,), (0,))
NT = ((1,), (1,))
TN = ((0,), (0,))


def split3(v):
    hi = v.astype(BF16).astype(F32)
    mid = (v - hi).astype(BF16).astype(F32)
    low = (v - hi - mid).astype(BF16).astype(F32)
    return hi, mid, low


def turned(rows, third):
    cut = THIRD * third
    return rows if cut == 0 else jnp.concatenate([rows[cut:TOK], rows[:cut]], axis=0)


def pack_kernel(scal, stale, stream, frames, out, aux, frame_row):
    step = pl.program_id(0)
    section = scal[0]

    @pl.when(step == 0)
    def _():
        frame_row[...] = jnp.zeros((8, 128), F32)
        frame_row[0:1, 0:TOK] = frames[...].astype(F32)
        square = jnp.zeros((TOK, 128), F32)
        for head in range(HEADS):
            part = stream[:, 128 * head : 128 * head + 128].astype(F32)
            square = square + part * part
        square = jnp.concatenate([square, jnp.zeros((8, 128), F32)], axis=0)
        total = jnp.sum(square.T, axis=0, keepdims=True)
        r = lax.rsqrt(total * (1.0 / WIDTH) + EPSILON)
        hi, mid, low = split3(jnp.broadcast_to(r, (8, 128)))
        row = lax.broadcasted_iota(jnp.int32, (8, 128), 0)
        lane = lax.broadcasted_iota(jnp.int32, (8, 128), 1)
        a = jnp.where(row == 0, hi, jnp.where(row == 1, mid, jnp.where(row == 2, low, 0.0)))
        a = jnp.where(row == 3, frame_row[0:1, :], a)
        a = jnp.where(lane < TOK, a, 0.0)
        aux[0] = a
        for third in range(1, 3):
            cut = THIRD * third
            t = jnp.where(lane < TOK - cut, pltpu.roll(a, 128 - cut, 1), pltpu.roll(a, TOK - cut, 1))
            aux[third] = jnp.where(lane < TOK, t, 0.0)

    none = jnp.zeros((8, 128), F32)

    def blocks(head):
        cols = pl.ds(pl.multiple_of(head * 128, 128), 128)
        keys = stale[0, :, cols].astype(F32)
        vals = jnp.concatenate([stale[1, :, cols].astype(F32), none], axis=0).T.astype(BF16)
        x = stream[:, cols].astype(F32)
        halves = []
        for third in range(3):
            t = turned(x, third)
            halves.append(jnp.where(section == 0, t[0:64], t[TOK - 64 : TOK]).astype(BF16))
        return keys, vals, halves

    def put(at, keys, vals, x, third):
        out[at, 0:128] = jnp.concatenate([keys, aux[third]], axis=0).astype(BF16)
        out[at, 128:256] = vals
        out[at, 256:CHUNK] = x

    more_keys, more_vals, more_x = blocks(16 + step)
    for y in range(4):
        keys, vals, halves = blocks(4 * step + y)
        for third in range(3):
            put(4 * y + third, keys, vals, halves[third], third)
        put(4 * y + 3, more_keys, more_vals, more_x[y % 3], y % 3)


def pack(section, stale, stream, frames):
    grid = pltpu.PrefetchScalarGridSpec(
        num_scalar_prefetch=1,
        grid=(4,),
        in_specs=[
            pl.BlockSpec((2, TOK, WIDTH), lambda r, s: (0, 0, 0)),
            pl.BlockSpec((TOK, WIDTH), lambda r, s: (0, 0)),
            pl.BlockSpec((1, TOK), lambda r, s: (0, 0)),
        ],
        out_specs=pl.BlockSpec((16, CHUNK, 128), lambda r, s: (r, 0, 0)),
        scratch_shapes=[pltpu.VMEM((3, 8, 128), F32), pltpu.VMEM((8, 128), F32)],
    )
    return pl.pallas_call(
        pack_kernel,
        grid_spec=grid,
        out_shape=jax.ShapeDtypeStruct((64, CHUNK, 128), BF16),
        compiler_params=PARAMS,
        name="pack",
    )(section, stale, stream, frames)


def mod_table(frame_mod, with_scale):
    hi, mid, low = split3(frame_mod)
    table = jnp.concatenate([hi, mid, low, jnp.zeros((16, frame_mod.shape[1]), F32)], axis=0)
    if with_scale:
        row = lax.broadcasted_iota(jnp.int32, (64, 128), 0)
        extra = jnp.where((row >= 48) & (row < 51), 1.0, 0.0)
        table = jnp.concatenate([table, extra], axis=1)
    return table.astype(BF16)


def hot_rows(aux):
    row = lax.broadcasted_iota(jnp.int32, (48, 128), 0)
    hot = jnp.where((row & 15).astype(F32) == aux[3:4, :], 1.0, 0.0)
    return jnp.concatenate([hot, aux, jnp.zeros((8, 128), F32)], axis=0).astype(BF16)


def modulations(kv, table, mods):
    for begin in range(0, PATCHES, 8):
        hot = [hot_rows(kv[0, p, 112:128, :].astype(F32)[8:16]) for p in range(begin, begin + 8)]
        at = slice(begin * 128, begin * 128 + 1024)
        mods[at, 0 : table.shape[1]] = dot(jnp.concatenate(hot, axis=1), table, TN)


def place_pair(t, hids, maps, kv, qa, ka, vt, kf, vh):
    row = lax.broadcasted_iota(jnp.int32, (80, 128), 0)
    col = lax.broadcasted_iota(jnp.int32, (80, 128), 1)
    patch = 2 * t + jnp.where(row >= THIRD, 1, 0)
    at = slice(t * 80, t * 80 + 80)
    q = jnp.concatenate([hid[0:THIRD] for hid in hids], axis=0) * maps[0:1, :]
    qa[at, 0:128] = q.astype(BF16)
    qa[at, 128:256] = jnp.where((col == patch) | (col == PATCHES), 1.0, 0.0).astype(BF16)
    row = lax.broadcasted_iota(jnp.int32, (128, 128), 0)
    col = lax.broadcasted_iota(jnp.int32, (128, 128), 1)
    for half in range(2):
        p = 2 * t + half
        at = slice(p * 128, p * 128 + 128)
        ka[at, 0:128] = kv[0, p, 0:128, :]
        hidden = (col == p) | ((col == PATCHES) & (row >= TOK))
        ka[at, 128:256] = jnp.where(hidden, -BIG, 0.0).astype(BF16)
        vt[0:128, at] = kv[0, p, 128:256, :]
        kf[at, 0:128] = (hids[half] * maps[1:2, :]).astype(BF16)
        hidden = (col <= PATCHES) & ((row >= TOK) | ((col != p) & (col < PATCHES)))
        kf[at, 128:256] = jnp.where(hidden, -BIG, 0.0).astype(BF16)
        vh[at, :] = (hids[half] * maps[2:3, :]).astype(BF16)


def turn_values(vh, vt, vf):
    row = lax.broadcasted_iota(jnp.int32, (128, 128), 0)
    col = lax.broadcasted_iota(jnp.int32, (128, 128), 1)
    unit = jnp.where(row == col, 1.0, 0.0).astype(BF16)
    for begin in range(0, PATCHES * 128, 1024):
        at = slice(begin, begin + 1024)
        vf[0:128, at] = dot(unit, vh[at, :], NT).astype(BF16)
    vt[128:144, :] = jnp.ones((16, PATCHES * 128), BF16)
    vf[128:144, :] = jnp.ones((16, PATCHES * 128), BF16)


def norms(ref):
    ones = jnp.ones((8, 128), BF16)
    parts = []
    for begin in range(0, ref.shape[0], 640 if ref.shape[0] % 1024 else 1024):
        at = slice(begin, begin + (640 if ref.shape[0] % 1024 else 1024))
        v = ref[at, 0:128].astype(F32)
        parts.append(dot(ones, (v * v).astype(BF16), NT))
    return jnp.concatenate(parts, axis=1) * 1.01


def attention(qa, ka, vt, kf, vf, xo, go, sc, pt, result):
    step = 512
    stale = PATCHES * 128
    keys = stale + step
    row = lax.broadcasted_iota(jnp.int32, (128, 256), 0)
    col = lax.broadcasted_iota(jnp.int32, (128, 256), 1)
    unit = jnp.where((row == col) | (row + 128 == col), 1.0, 0.0).astype(BF16)

    def fresh_at(lane):
        low = lane // TILE * (TILE // THIRD) + lane % TILE // 128 * 3
        return slice(low * 128, low * 128 + step)

    def scores(first, width, begin):
        if begin < stale:
            return dot(ka[begin : begin + step, :], qa[first : first + width, :], NT)
        lanes = range(first, first + width, 128)
        parts = [dot(kf[fresh_at(lane), :], qa[lane : lane + 128, :], NT) for lane in lanes]
        return jnp.concatenate(parts, axis=1)

    def weigh(first, width, begin, s, top):
        weights = jnp.exp2((s - top) * FACTOR).astype(BF16)
        pt[begin : begin + step, first : first + width] = weights

    def finish(first, width):
        total = dot(vt[...], pt[0:stale, first : first + width], NN)
        lanes = range(first, first + width, 128)
        more = [dot(vf[:, fresh_at(lane)], pt[stale:keys, lane : lane + 128], NN) for lane in lanes]
        total = total + jnp.concatenate(more, axis=1)
        mean = total[0:128] / total[128:129]
        hi = mean.astype(BF16)
        low = (mean - hi.astype(F32)).astype(BF16)
        for lane in lanes:
            cols = slice(lane - first, lane - first + 128)
            attended = dot(unit, jnp.concatenate([hi[:, cols], low[:, cols]], axis=1), NT)
            at = slice(lane, lane + 128)
            result(at, (xo[at, :] + go[at, :] * attended).astype(BF16))
        return jnp.min(total[128:129])

    lane = lax.broadcasted_iota(jnp.int32, (8, stale), 1)
    longest = jnp.where((lane & 127) < TOK, jnp.maximum(norms(ka), norms(kf)), 0.0)
    longest = jnp.max(longest, axis=1, keepdims=True)[0:1]
    bound = jnp.sqrt(norms(qa)[0:1] * longest)
    least = None
    for first in range(0, OWN_ROWS, WIDE):
        top = bound[:, first : first + WIDE]
        for begin in range(0, keys, step):
            weigh(first, WIDE, begin, scores(first, WIDE, begin), top)
        here = finish(first, WIDE)
        least = here if least is None else jnp.minimum(least, here)

    @pl.when(jnp.logical_not(least > SMALL))
    def _():
        for first in range(0, OWN_ROWS, TILE):
            top = None
            for begin in range(0, keys, step):
                s = scores(first, TILE, begin)
                sc[begin : begin + step, :] = s
                here = jnp.max(s.reshape(step // 8, 8, TILE), axis=0)
                top = here if top is None else jnp.maximum(top, here)
            top = jnp.max(top, axis=0, keepdims=True)
            for begin in range(0, keys, step):
                weigh(first, TILE, begin, sc[begin : begin + step, :], top)
            finish(first, TILE)


def first_kernel(kv, x_rest, frame_mod, maps, x_out, sums, qa, ka, vt, kf, vf, xo, go, sc, pt, mods, vh, sq):
    table = mod_table(frame_mod[...], True)
    gains = maps[...]

    modulations(kv, table, mods)
    for t in range(PATCHES // 2):
        at = slice(t * 80, t * 80 + 80)
        hids, xs, gates = [], [], []
        for half in range(2):
            p = 2 * t + half
            xa = kv[0, p, 256:CHUNK, :].astype(F32)
            xb = x_rest[0, p].astype(F32)[8:64]
            x = jnp.concatenate([xa, xb, jnp.zeros((8, 128), F32)], axis=0)
            m = mods[p * 128 : p * 128 + 128, :]
            hids.append(x * m[:, 384:512] * (1.0 + m[:, 128:256]) + m[:, 0:128])
            xs.append(x[0:THIRD])
            gates.append(m[0:THIRD, 256:384])
        place_pair(t, hids, gains, kv, qa, ka, vt, kf, vh)
        xo[at, :] = jnp.concatenate(xs, axis=0)
        go[at, :] = jnp.concatenate(gates, axis=0)
    turn_values(vh, vt, vf)

    def result(at, value):
        x_out[at, :] = value
        wide = value.astype(F32)
        sq[at, :] = wide * wide

    attention(qa, ka, vt, kf, vf, xo, go, sc, pt, result)
    square = sq[...]
    hi = square.astype(BF16)
    low = (square - hi.astype(F32)).astype(BF16)
    ones = jnp.ones((8, 128), BF16)
    total = dot(ones, hi, NT) + dot(ones, low, NT)
    sums[...] = total


def mid_kernel(x, total, mid):
    hi = total[...].astype(BF16).astype(F32)
    low = total[...] - hi
    rows = [part[0:1, 128 * i : 128 * i + 128] for part in (hi, low) for i in range(10)]
    sums = jnp.concatenate(rows + [jnp.zeros((4, 128), F32)], axis=0)
    for t in range(PATCHES // 2):
        pair = x[80 * t : 80 * t + 80, :].astype(F32)
        for half in range(2):
            p = 2 * t + half
            block = jnp.concatenate([pair[THIRD * half : THIRD * half + THIRD], sums], axis=0).astype(BF16)
            mid[p] = block
            mid[PATCHES + p] = block


def middle(x, total):
    whole = pl.BlockSpec(memory_space=pltpu.VMEM)
    return pl.pallas_call(
        mid_kernel,
        in_specs=[whole, whole],
        out_specs=whole,
        out_shape=jax.ShapeDtypeStruct((64, MID, 128), BF16),
        compiler_params=PARAMS,
        name="middle",
    )(x, total)


SCRATCH = [
    pltpu.VMEM((OWN_ROWS, 256), BF16),
    pltpu.VMEM((PATCHES * 128, 256), BF16),
    pltpu.VMEM((144, PATCHES * 128), BF16),
    pltpu.VMEM((PATCHES * 128, 256), BF16),
    pltpu.VMEM((144, PATCHES * 128), BF16),
    pltpu.VMEM((OWN_ROWS, 128), F32),
    pltpu.VMEM((OWN_ROWS, 128), F32),
    pltpu.VMEM((PATCHES * 128 + 512, TILE), F32),
    pltpu.VMEM((PATCHES * 128 + 512, OWN_ROWS), BF16),
    pltpu.VMEM((PATCHES * 128, 512), F32),
    pltpu.VMEM((PATCHES * 128, 128), BF16),
]


def first_layer(received, frame_mod, maps):
    return pl.pallas_call(
        first_kernel,
        grid=(1,),
        in_specs=[
            pl.BlockSpec((1, PATCHES, CHUNK, 128), lambda i: (0, 0, 0, 0)),
            pl.BlockSpec((1, PATCHES, 64, 128), lambda i: (1, 0, 4, 0)),
            pl.BlockSpec((16, 384), lambda i: (0, 0)),
            pl.BlockSpec((3, 128), lambda i: (0, 0)),
        ],
        out_specs=[
            pl.BlockSpec((OWN_ROWS, 128), lambda i: (0, 0)),
            pl.BlockSpec((8, OWN_ROWS), lambda i: (0, 0)),
        ],
        out_shape=[
            jax.ShapeDtypeStruct((OWN_ROWS, 128), BF16),
            jax.ShapeDtypeStruct((8, OWN_ROWS), F32),
        ],
        scratch_shapes=SCRATCH + [pltpu.VMEM((OWN_ROWS, 128), F32)],
        compiler_params=PARAMS,
        name="first_layer",
    )(received, received, frame_mod, maps)


def second_kernel(scal, kv, own, after, before, sums, frame_mod, maps, x_out, qa, ka, vt, kf, vf, xo, go, sc, pt, mods, vh, rs):
    table = mod_table(frame_mod[...], False)
    gains = maps[...]
    third = scal[0]
    row = lax.broadcasted_iota(jnp.int32, (16, OWN_ROWS), 0)
    ones = jnp.where(lax.broadcasted_iota(jnp.int32, (16, 128), 0) < 3, 1.0, 0.0).astype(BF16)
    for k in range(3):
        which = lax.rem(third + k, 3)
        total = None
        for head in range(HEADS):
            at = 4 * head + which if head < 16 else 16 * (head - 16) + 4 * which + 3
            part = sums[at].astype(F32)
            total = part if total is None else total + part
        square = jnp.concatenate([total[8 + i : 9 + i] + total[18 + i : 19 + i] for i in range(10)], axis=1)
        hi, mid, low = split3(lax.rsqrt(square * (1.0 / WIDTH) + EPSILON))
        r = jnp.where(row == 0, hi, jnp.where(row == 1, mid, jnp.where(row == 2, low, 0.0)))
        rs[k] = dot(r.astype(BF16), ones, TN)

    modulations(kv, table, mods)
    for t in range(PATCHES // 2):
        at = slice(t * 80, t * 80 + 80)
        pair = [ref[at, :].astype(F32) for ref in (own, after, before)]
        scale = [rs[k, at, :] for k in range(3)]
        hids, gates = [], []
        for half in range(2):
            p = 2 * t + half
            cut = slice(THIRD * half, THIRD * half + THIRD)
            none = [jnp.zeros((8, 128), F32)]
            x = jnp.concatenate([v[cut] for v in pair] + none, axis=0)
            r = jnp.concatenate([v[cut] for v in scale] + none, axis=0)
            m = mods[p * 128 : p * 128 + 128, 0:384]
            hids.append(x * r * (1.0 + m[:, 128:256]) + m[:, 0:128])
            gates.append(m[0:THIRD, 256:384])
        place_pair(t, hids, gains, kv, qa, ka, vt, kf, vh)
        xo[at, :] = pair[0]
        go[at, :] = jnp.concatenate(gates, axis=0)
    turn_values(vh, vt, vf)

    def result(at, value):
        x_out[at, :] = value

    attention(qa, ka, vt, kf, vf, xo, go, sc, pt, result)


def second_layer(third, received, own, after, before, sums, frame_mod, maps):
    rows = pl.BlockSpec((OWN_ROWS, 128), lambda i, s: (0, 0))
    grid = pltpu.PrefetchScalarGridSpec(
        num_scalar_prefetch=1,
        grid=(1,),
        in_specs=[
            pl.BlockSpec((1, PATCHES, 256, 128), lambda i, s: (1, 0, 0, 0)),
            rows,
            rows,
            rows,
            pl.BlockSpec((64, 32, 128), lambda i, s: (0, 1, 0)),
            pl.BlockSpec((16, 384), lambda i, s: (0, 0)),
            pl.BlockSpec((3, 128), lambda i, s: (0, 0)),
        ],
        out_specs=rows,
        scratch_shapes=SCRATCH + [pltpu.VMEM((3, OWN_ROWS, 128), F32)],
    )
    return pl.pallas_call(
        second_kernel,
        grid_spec=grid,
        out_shape=jax.ShapeDtypeStruct((OWN_ROWS, 128), BF16),
        compiler_params=PARAMS,
        name="second_layer",
    )(third, received, own, after, before, sums, frame_mod, maps)


def home_kernel(scal, got, stream, frames, frame_mod, maps, out, xs, frame_row):
    section = scal[0]
    frame_row[0:1, 0:TOK] = frames[...].astype(F32)
    square = jnp.zeros((TOK, 128), F32)
    for head in range(HEADS):
        cols = slice(128 * head, 128 * head + 128)
        parts = [got[place_of(head, third)].astype(F32)[0:THIRD] for third in range(3)]
        x = jnp.where(section == 0, stream[:, cols].astype(F32), jnp.concatenate(parts, axis=0))
        xs[:, cols] = x
        square = square + x * x
    r = lax.rsqrt(jnp.sum(square, axis=1, keepdims=True) * (1.0 / WIDTH) + EPSILON)
    row = lax.broadcasted_iota(jnp.int32, (48, 128), 0)
    hot = jnp.where((row & 15).astype(F32) == frame_row[0:1, :], 1.0, 0.0).astype(BF16)
    for head in range(HEADS):
        cols = slice(128 * head, 128 * head + 128)
        more = slice(WIDTH + 128 * head, WIDTH + 128 * head + 128)
        mod = jnp.concatenate([frame_mod[:, cols], frame_mod[:, more]], axis=1)
        m = dot(hot, jnp.concatenate(split3(mod), axis=0).astype(BF16), TN)[0:TOK]
        hid = xs[:, cols] * r * (1.0 + m[:, 128:256]) + m[:, 0:128]
        out[0, :, cols] = (hid * maps[1:2, cols]).astype(BF16)
        out[1, :, cols] = (hid * maps[2:3, cols]).astype(BF16)


def home(section, got, stream, frames, frame_mod, maps):
    whole = pl.BlockSpec(memory_space=pltpu.VMEM)
    return pl.pallas_call(
        home_kernel,
        in_specs=[pl.BlockSpec(memory_space=pltpu.SMEM)] + [whole] * 5,
        out_specs=whole,
        out_shape=jax.ShapeDtypeStruct((2, TOK, WIDTH), BF16),
        scratch_shapes=[pltpu.VMEM((TOK, WIDTH), F32), pltpu.VMEM((8, 128), F32)],
        compiler_params=PARAMS,
        name="home",
    )(section, got, stream, frames, frame_mod, maps)


def unpack_kernel(scal, got, out):
    branch = scal[0]
    for j in range(HEADS // 2):
        parts = []
        for third in range(3):
            a, b = place_of(j, third), place_of(j + HEADS // 2, third)
            parts.append(got[jnp.where(branch == 0, a, b)].astype(F32))
        out[:, 128 * j : 128 * j + 128] = jnp.concatenate(parts, axis=0).astype(BF16)


def unpack(branch, got):
    whole = pl.BlockSpec(memory_space=pltpu.VMEM)
    return pl.pallas_call(
        unpack_kernel,
        in_specs=[pl.BlockSpec(memory_space=pltpu.SMEM), whole],
        out_specs=whole,
        out_shape=jax.ShapeDtypeStruct((TOK, WIDTH // 2), BF16),
        compiler_params=PARAMS,
        name="unpack",
    )(branch, got)


def body(stream, token_frame, frame_levels, level_table, branch_mod, layer_mod, maps, stale_kv):
    section = lax.axis_index("section")
    branch = lax.axis_index("branch")
    place = section * PATCHES + lax.axis_index("patch")
    x, y, z = place % 4, (place // 4) % 4, place // 16
    head = jnp.where(x < 3, place // 4, 16 + z)
    third = jnp.where(x < 3, x, jnp.where(y < 3, y, 0))

    both = jnp.concatenate([layer_mod.reshape(3, WIDTH), maps[0]], axis=0)
    other = lax.ppermute(both, "section", [(0, 1), (1, 0)])

    frames = token_frame.reshape(1, TOK)
    section_at = section.reshape(1).astype(jnp.int32)
    send = pack(section_at, stale_kv[0, 0], stream, frames)
    received = lax.all_to_all(send, PLANE, 0, 0, tiled=True)
    received = received.reshape(2, PATCHES, CHUNK, 128)

    level_hot = (frame_levels[:, None] == jnp.arange(LEVELS, dtype=jnp.int32)[None, :]).astype(F32)
    base = jnp.dot(level_hot, level_table, precision=lax.Precision.HIGHEST, preferred_element_type=F32)
    home_mod = base + (layer_mod[0] + branch_mod[0])[None, :]

    def of_head(array):
        rows = array.shape[0]
        return lax.dynamic_slice_in_dim(array.reshape(rows, -1, HEADS, 128), head, 1, 2)[:, :, 0]

    layers = jnp.stack([jnp.where(section == 0, both, other), jnp.where(section == 0, other, both)])
    mine = of_head(layers.reshape(12, WIDTH)).reshape(2, 6, 128)
    base_mine = of_head(base)
    branch_mine = of_head(branch_mod)[0]
    mods = base_mine[None] + (mine[:, 0:3] + branch_mine[None])[:, None]
    mods = mods.reshape(2, FRAMES, 384)
    gains = mine[:, 3:6]

    x_one, total = first_layer(received, mods[0], gains[0])

    def from_third(by):
        pairs = [(place_of(h, (g + by) % 3), place_of(h, g)) for h in range(HEADS) for g in range(3)]
        return lax.ppermute(x_one, PLANE, pairs)

    after, before = from_third(1), from_third(2)
    mid = middle(x_one, total)
    mid_got = lax.all_to_all(mid, PLANE, 0, 0, tiled=True)
    fresh = home(section_at, mid_got, stream, frames, home_mod, maps[0])
    x_two = second_layer(third.reshape(1).astype(jnp.int32), received, x_one, after, before, mid_got, mods[1], gains[1])

    x_other = lax.ppermute(x_two, "branch", [(0, 1), (1, 0)])
    cond = jnp.where(branch == 0, x_two, x_other).astype(F32)
    uncond = jnp.where(branch == 0, x_other, x_two).astype(F32)
    guided = (uncond + GUIDE * (cond - uncond)).astype(BF16).reshape(1, PATCHES, THIRD, 128)
    guided = jnp.broadcast_to(guided, (2, PATCHES, THIRD, 128)).reshape(64, THIRD, 128)
    guided_got = lax.all_to_all(guided, PLANE, 0, 0, tiled=True)
    out = unpack(branch.reshape(1).astype(jnp.int32), guided_got)
    return (out, fresh[None, None])


def solution(mesh):
    placed = (
        P("patch", None),
        P("patch"),
        P(),
        P(),
        P("branch", None),
        P("section", None),
        P("section", None, None),
        P("branch", "section", None, "patch", None),
    )
    return jax.shard_map(
        body,
        mesh=mesh,
        in_specs=placed,
        out_specs=(P("patch", "branch"), P("branch", "section", None, "patch", None)),
        check_vma=False,
    )
```

```python
import functools
import math

import jax
import jax.numpy as jnp
from jax import lax
from jax.experimental import pallas as pl
from jax.experimental.pallas import tpu as pltpu
from jax.sharding import PartitionSpec as P

HEADS = 20
HEAD_DIM = 128
FRAMES = 16
LEVELS = 50
TOK = 120
THIRD = 40
PATCHES = 32
WIDTH = HEADS * HEAD_DIM
EPSILON = 1e-06
GUIDE = 5.0
BIG = 1e30
PLANE = ("section", "patch")
F32 = jnp.float32
BF16 = jnp.bfloat16
VMEM_BYTES = 56 * 1024 * 1024
PARAMS = pltpu.CompilerParams(vmem_limit_bytes=VMEM_BYTES)

OWN_ROWS = PATCHES * THIRD
TILE = 640
WIDE = 1280
SMALL = 1e-25
FACTOR = HEAD_DIM ** (-0.5) * math.log2(math.e)
CHUNK = 320
MID = 64


def place_of(head, third):
    if head < 16:
        return 4 * head + third
    return 16 * (head - 16) + 4 * third + 3


def dot(a, b, dims):
    return lax.dot_general(a, b, (dims, ((), ())), preferred_element_type=F32)


NN = ((1,), (0,))
NT = ((1,), (1,))
TN = ((0,), (0,))


def split3(v):
    hi = v.astype(BF16).astype(F32)
    mid = (v - hi).astype(BF16).astype(F32)
    low = (v - hi - mid).astype(BF16).astype(F32)
    return hi, mid, low


def turned(rows, third):
    cut = THIRD * third
    return rows if cut == 0 else jnp.concatenate([rows[cut:TOK], rows[:cut]], axis=0)


def pack_kernel(scal, stale, stream, frames, out, aux, frame_row):
    step = pl.program_id(0)
    section = scal[0]

    @pl.when(step == 0)
    def _():
        frame_row[...] = jnp.zeros((8, 128), F32)
        frame_row[0:1, 0:TOK] = frames[...].astype(F32)
        square = jnp.zeros((TOK, 128), F32)
        for head in range(HEADS):
            part = stream[:, 128 * head : 128 * head + 128].astype(F32)
            square = square + part * part
        square = jnp.concatenate([square, jnp.zeros((8, 128), F32)], axis=0)
        total = jnp.sum(square.T, axis=0, keepdims=True)
        r = lax.rsqrt(total * (1.0 / WIDTH) + EPSILON)
        hi, mid, low = split3(jnp.broadcast_to(r, (8, 128)))
        row = lax.broadcasted_iota(jnp.int32, (8, 128), 0)
        lane = lax.broadcasted_iota(jnp.int32, (8, 128), 1)
        a = jnp.where(row == 0, hi, jnp.where(row == 1, mid, jnp.where(row == 2, low, 0.0)))
        a = jnp.where(row == 3, frame_row[0:1, :], a)
        a = jnp.where(lane < TOK, a, 0.0)
        aux[0] = a
        for third in range(1, 3):
            cut = THIRD * third
            t = jnp.where(lane < TOK - cut, pltpu.roll(a, 128 - cut, 1), pltpu.roll(a, TOK - cut, 1))
            aux[third] = jnp.where(lane < TOK, t, 0.0)

    none = jnp.zeros((8, 128), F32)

    def blocks(head):
        cols = pl.ds(pl.multiple_of(head * 128, 128), 128)
        keys = stale[0, :, cols].astype(F32)
        vals = jnp.concatenate([stale[1, :, cols].astype(F32), none], axis=0).T.astype(BF16)
        x = stream[:, cols].astype(F32)
        halves = []
        for third in range(3):
            t = turned(x, third)
            halves.append(jnp.where(section == 0, t[0:64], t[TOK - 64 : TOK]).astype(BF16))
        return keys, vals, halves

    def put(at, keys, vals, x, third):
        out[at, 0:128] = jnp.concatenate([keys, aux[third]], axis=0).astype(BF16)
        out[at, 128:256] = vals
        out[at, 256:CHUNK] = x

    more_keys, more_vals, more_x = blocks(16 + step)
    for y in range(4):
        keys, vals, halves = blocks(4 * step + y)
        for third in range(3):
            put(4 * y + third, keys, vals, halves[third], third)
        put(4 * y + 3, more_keys, more_vals, more_x[y % 3], y % 3)


def pack(section, stale, stream, frames):
    grid = pltpu.PrefetchScalarGridSpec(
        num_scalar_prefetch=1,
        grid=(4,),
        in_specs=[
            pl.BlockSpec((2, TOK, WIDTH), lambda r, s: (0, 0, 0)),
            pl.BlockSpec((TOK, WIDTH), lambda r, s: (0, 0)),
            pl.BlockSpec((1, TOK), lambda r, s: (0, 0)),
        ],
        out_specs=pl.BlockSpec((16, CHUNK, 128), lambda r, s: (r, 0, 0)),
        scratch_shapes=[pltpu.VMEM((3, 8, 128), F32), pltpu.VMEM((8, 128), F32)],
    )
    return pl.pallas_call(
        pack_kernel,
        grid_spec=grid,
        out_shape=jax.ShapeDtypeStruct((64, CHUNK, 128), BF16),
        compiler_params=PARAMS,
        name="pack",
    )(section, stale, stream, frames)


def mod_table(frame_mod, with_scale):
    hi, mid, low = split3(frame_mod)
    table = jnp.concatenate([hi, mid, low, jnp.zeros((16, frame_mod.shape[1]), F32)], axis=0)
    if with_scale:
        row = lax.broadcasted_iota(jnp.int32, (64, 128), 0)
        extra = jnp.where((row >= 48) & (row < 51), 1.0, 0.0)
        table = jnp.concatenate([table, extra], axis=1)
    return table.astype(BF16)


def hot_rows(aux):
    row = lax.broadcasted_iota(jnp.int32, (48, 128), 0)
    hot = jnp.where((row & 15).astype(F32) == aux[3:4, :], 1.0, 0.0)
    return jnp.concatenate([hot, aux, jnp.zeros((8, 128), F32)], axis=0).astype(BF16)


def modulations(kv, table, mods):
    for begin in range(0, PATCHES, 8):
        hot = [hot_rows(kv[0, p, 112:128, :].astype(F32)[8:16]) for p in range(begin, begin + 8)]
        at = slice(begin * 128, begin * 128 + 1024)
        mods[at, 0 : table.shape[1]] = dot(jnp.concatenate(hot, axis=1), table, TN)


def place_pair(t, hids, maps, kv, qa, ka, vt, kf, vh):
    row = lax.broadcasted_iota(jnp.int32, (80, 128), 0)
    col = lax.broadcasted_iota(jnp.int32, (80, 128), 1)
    patch = 2 * t + jnp.where(row >= THIRD, 1, 0)
    at = slice(t * 80, t * 80 + 80)
    q = jnp.concatenate([hid[0:THIRD] for hid in hids], axis=0) * maps[0:1, :]
    qa[at, 0:128] = q.astype(BF16)
    qa[at, 128:256] = jnp.where((col == patch) | (col == PATCHES), 1.0, 0.0).astype(BF16)
    row = lax.broadcasted_iota(jnp.int32, (128, 128), 0)
    col = lax.broadcasted_iota(jnp.int32, (128, 128), 1)
    for half in range(2):
        p = 2 * t + half
        at = slice(p * 128, p * 128 + 128)
        ka[at, 0:128] = kv[0, p, 0:128, :]
        hidden = (col == p) | ((col == PATCHES) & (row >= TOK))
        ka[at, 128:256] = jnp.where(hidden, -BIG, 0.0).astype(BF16)
        vt[0:128, at] = kv[0, p, 128:256, :]
        kf[at, 0:128] = (hids[half] * maps[1:2, :]).astype(BF16)
        hidden = (col <= PATCHES) & ((row >= TOK) | ((col != p) & (col < PATCHES)))
        kf[at, 128:256] = jnp.where(hidden, -BIG, 0.0).astype(BF16)
        vh[at, :] = (hids[half] * maps[2:3, :]).astype(BF16)


def turn_values(vh, vt, vf):
    row = lax.broadcasted_iota(jnp.int32, (128, 128), 0)
    col = lax.broadcasted_iota(jnp.int32, (128, 128), 1)
    unit = jnp.where(row == col, 1.0, 0.0).astype(BF16)
    for begin in range(0, PATCHES * 128, 1024):
        at = slice(begin, begin + 1024)
        vf[0:128, at] = dot(unit, vh[at, :], NT).astype(BF16)
    vt[128:144, :] = jnp.ones((16, PATCHES * 128), BF16)
    vf[128:144, :] = jnp.ones((16, PATCHES * 128), BF16)


def norms(ref):
    ones = jnp.ones((8, 128), BF16)
    parts = []
    for begin in range(0, ref.shape[0], 640 if ref.shape[0] % 1024 else 1024):
        at = slice(begin, begin + (640 if ref.shape[0] % 1024 else 1024))
        v = ref[at, 0:128].astype(F32)
        parts.append(dot(ones, (v * v).astype(BF16), NT))
    return jnp.concatenate(parts, axis=1) * 1.01


def attention(qa, ka, vt, kf, vf, xo, go, sc, pt, result):
    step = 512
    stale = PATCHES * 128
    keys = stale + step
    row = lax.broadcasted_iota(jnp.int32, (128, 256), 0)
    col = lax.broadcasted_iota(jnp.int32, (128, 256), 1)
    unit = jnp.where((row == col) | (row + 128 == col), 1.0, 0.0).astype(BF16)

    def fresh_at(lane):
        low = lane // TILE * (TILE // THIRD) + lane % TILE // 128 * 3
        return pl.ds(low * 128 if isinstance(low, int) else pl.multiple_of(low * 128, 128), step)

    def scores(first, width, begin):
        return dot(ka[pl.ds(begin, step), :], qa[pl.ds(first, width), :], NT)

    def fresh_scores(first, width):
        lanes = [first + i for i in range(0, width, 128)]
        parts = [dot(kf[fresh_at(lane), :], qa[pl.ds(lane, 128), :], NT) for lane in lanes]
        return jnp.concatenate(parts, axis=1)

    def weigh(first, width, begin, s, top):
        weights = jnp.exp2((s - top) * FACTOR).astype(BF16)
        pt[pl.ds(begin, step), pl.ds(first, width)] = weights

    def finish(first, width):
        total = dot(vt[...], pt[0:stale, pl.ds(first, width)], NN)
        lanes = [first + i for i in range(0, width, 128)]
        more = [dot(vf[:, fresh_at(lane)], pt[stale:keys, pl.ds(lane, 128)], NN) for lane in lanes]
        total = total + jnp.concatenate(more, axis=1)
        mean = total[0:128] / total[128:129]
        hi = mean.astype(BF16)
        low = (mean - hi.astype(F32)).astype(BF16)
        for i, lane in enumerate(lanes):
            cols = slice(128 * i, 128 * i + 128)
            attended = dot(unit, jnp.concatenate([hi[:, cols], low[:, cols]], axis=1), NT)
            at = pl.ds(lane, 128)
            result(at, (xo[at, :] + go[at, :] * attended).astype(BF16))
        return jnp.min(total[128:129])

    lane = lax.broadcasted_iota(jnp.int32, (8, stale), 1)
    longest = jnp.where((lane & 127) < TOK, jnp.maximum(norms(ka), norms(kf)), 0.0)
    longest = jnp.max(longest, axis=1, keepdims=True)[0:1]
    bound = jnp.sqrt(norms(qa)[0:1] * longest)
    least = None
    for first in range(0, OWN_ROWS, WIDE):
        top = bound[:, first : first + WIDE]
        for begin in range(0, stale, step):
            weigh(first, WIDE, begin, scores(first, WIDE, begin), top)
        weigh(first, WIDE, stale, fresh_scores(first, WIDE), top)
        here = finish(first, WIDE)
        least = here if least is None else jnp.minimum(least, here)

    @pl.when(jnp.logical_not(least > SMALL))
    def _():
        @pl.loop(0, OWN_ROWS // TILE)
        def _(tile):
            first = pl.multiple_of(tile * TILE, 128)
            s = fresh_scores(first, TILE)
            sc[stale:keys, :] = s

            def one(i, top):
                begin = pl.multiple_of(i * step, step)
                s = scores(first, TILE, begin)
                sc[pl.ds(begin, step), :] = s
                return jnp.maximum(top, jnp.max(s.reshape(step // 8, 8, TILE), axis=0))

            top = lax.fori_loop(0, stale // step, one, jnp.max(s.reshape(step // 8, 8, TILE), axis=0))
            top = jnp.max(top, axis=0, keepdims=True)

            @pl.loop(0, keys // step)
            def _(i):
                begin = pl.multiple_of(i * step, step)
                weigh(first, TILE, begin, sc[pl.ds(begin, step), :], top)

            finish(first, TILE)


def first_kernel(kv, x_rest, frame_mod, maps, x_out, mid, qa, ka, vt, kf, vf, xo, go, sc, pt, mods, vh, sq):
    table = mod_table(frame_mod[...], True)
    gains = maps[...]

    modulations(kv, table, mods)
    for t in range(PATCHES // 2):
        at = slice(t * 80, t * 80 + 80)
        hids, xs, gates = [], [], []
        for half in range(2):
            p = 2 * t + half
            xa = kv[0, p, 256:CHUNK, :].astype(F32)
            xb = x_rest[0, p].astype(F32)[8:64]
            x = jnp.concatenate([xa, xb, jnp.zeros((8, 128), F32)], axis=0)
            m = mods[p * 128 : p * 128 + 128, :]
            hids.append(x * m[:, 384:512] * (1.0 + m[:, 128:256]) + m[:, 0:128])
            xs.append(x[0:THIRD])
            gates.append(m[0:THIRD, 256:384])
        place_pair(t, hids, gains, kv, qa, ka, vt, kf, vh)
        xo[at, :] = jnp.concatenate(xs, axis=0)
        go[at, :] = jnp.concatenate(gates, axis=0)
    turn_values(vh, vt, vf)

    def result(at, value):
        x_out[at, :] = value
        wide = value.astype(F32)
        sq[at, :] = wide * wide

    attention(qa, ka, vt, kf, vf, xo, go, sc, pt, result)
    square = sq[...]
    hi = square.astype(BF16)
    low = (square - hi.astype(F32)).astype(BF16)
    ones = jnp.ones((8, 128), BF16)
    total = dot(ones, hi, NT) + dot(ones, low, NT)
    hi = total.astype(BF16).astype(F32)
    low = total - hi
    rows = [part[0:1, 128 * i : 128 * i + 128] for part in (hi, low) for i in range(10)]
    sums = jnp.concatenate(rows + [jnp.zeros((4, 128), F32)], axis=0)
    for t in range(PATCHES // 2):
        pair = x_out[80 * t : 80 * t + 80, :].astype(F32)
        for half in range(2):
            p = 2 * t + half
            block = jnp.concatenate([pair[THIRD * half : THIRD * half + THIRD], sums], axis=0).astype(BF16)
            mid[p] = block
            mid[PATCHES + p] = block


SCRATCH = [
    pltpu.VMEM((OWN_ROWS, 256), BF16),
    pltpu.VMEM((PATCHES * 128, 256), BF16),
    pltpu.VMEM((144, PATCHES * 128), BF16),
    pltpu.VMEM((PATCHES * 128, 256), BF16),
    pltpu.VMEM((144, PATCHES * 128), BF16),
    pltpu.VMEM((OWN_ROWS, 128), F32),
    pltpu.VMEM((OWN_ROWS, 128), F32),
    pltpu.VMEM((PATCHES * 128 + 512, TILE), F32),
    pltpu.VMEM((PATCHES * 128 + 512, OWN_ROWS), BF16),
    pltpu.VMEM((PATCHES * 128, 512), F32),
    pltpu.VMEM((PATCHES * 128, 128), BF16),
]


def first_layer(received, frame_mod, maps):
    return pl.pallas_call(
        first_kernel,
        grid=(1,),
        in_specs=[
            pl.BlockSpec((1, PATCHES, CHUNK, 128), lambda i: (0, 0, 0, 0)),
            pl.BlockSpec((1, PATCHES, 64, 128), lambda i: (1, 0, 4, 0)),
            pl.BlockSpec((16, 384), lambda i: (0, 0)),
            pl.BlockSpec((3, 128), lambda i: (0, 0)),
        ],
        out_specs=[
            pl.BlockSpec((OWN_ROWS, 128), lambda i: (0, 0)),
            pl.BlockSpec((64, MID, 128), lambda i: (0, 0, 0)),
        ],
        out_shape=[
            jax.ShapeDtypeStruct((OWN_ROWS, 128), BF16),
            jax.ShapeDtypeStruct((64, MID, 128), BF16),
        ],
        scratch_shapes=SCRATCH + [pltpu.VMEM((OWN_ROWS, 128), F32)],
        compiler_params=PARAMS,
        name="first_layer",
    )(received, received, frame_mod, maps)


def second_kernel(scal, kv, own, after, before, sums, frame_mod, maps, x_out, qa, ka, vt, kf, vf, xo, go, sc, pt, mods, vh, rs):
    table = mod_table(frame_mod[...], False)
    gains = maps[...]
    third = scal[0]
    row = lax.broadcasted_iota(jnp.int32, (16, OWN_ROWS), 0)
    ones = jnp.where(lax.broadcasted_iota(jnp.int32, (16, 128), 0) < 3, 1.0, 0.0).astype(BF16)
    for k in range(3):
        which = lax.rem(third + k, 3)
        total = None
        for head in range(HEADS):
            at = 4 * head + which if head < 16 else 16 * (head - 16) + 4 * which + 3
            part = sums[at].astype(F32)
            total = part if total is None else total + part
        square = jnp.concatenate([total[8 + i : 9 + i] + total[18 + i : 19 + i] for i in range(10)], axis=1)
        hi, mid, low = split3(lax.rsqrt(square * (1.0 / WIDTH) + EPSILON))
        r = jnp.where(row == 0, hi, jnp.where(row == 1, mid, jnp.where(row == 2, low, 0.0)))
        rs[k] = dot(r.astype(BF16), ones, TN)

    modulations(kv, table, mods)
    for t in range(PATCHES // 2):
        at = slice(t * 80, t * 80 + 80)
        pair = [ref[at, :].astype(F32) for ref in (own, after, before)]
        scale = [rs[k, at, :] for k in range(3)]
        hids, gates = [], []
        for half in range(2):
            p = 2 * t + half
            cut = slice(THIRD * half, THIRD * half + THIRD)
            none = [jnp.zeros((8, 128), F32)]
            x = jnp.concatenate([v[cut] for v in pair] + none, axis=0)
            r = jnp.concatenate([v[cut] for v in scale] + none, axis=0)
            m = mods[p * 128 : p * 128 + 128, 0:384]
            hids.append(x * r * (1.0 + m[:, 128:256]) + m[:, 0:128])
            gates.append(m[0:THIRD, 256:384])
        place_pair(t, hids, gains, kv, qa, ka, vt, kf, vh)
        xo[at, :] = pair[0]
        go[at, :] = jnp.concatenate(gates, axis=0)
    turn_values(vh, vt, vf)

    def result(at, value):
        x_out[at, :] = value

    attention(qa, ka, vt, kf, vf, xo, go, sc, pt, result)


def second_layer(third, received, own, after, before, sums, frame_mod, maps):
    rows = pl.BlockSpec((OWN_ROWS, 128), lambda i, s: (0, 0))
    grid = pltpu.PrefetchScalarGridSpec(
        num_scalar_prefetch=1,
        grid=(1,),
        in_specs=[
            pl.BlockSpec((1, PATCHES, 256, 128), lambda i, s: (1, 0, 0, 0)),
            rows,
            rows,
            rows,
            pl.BlockSpec((64, 32, 128), lambda i, s: (0, 1, 0)),
            pl.BlockSpec((16, 384), lambda i, s: (0, 0)),
            pl.BlockSpec((3, 128), lambda i, s: (0, 0)),
        ],
        out_specs=rows,
        scratch_shapes=SCRATCH + [pltpu.VMEM((3, OWN_ROWS, 128), F32)],
    )
    return pl.pallas_call(
        second_kernel,
        grid_spec=grid,
        out_shape=jax.ShapeDtypeStruct((OWN_ROWS, 128), BF16),
        compiler_params=PARAMS,
        name="second_layer",
    )(third, received, own, after, before, sums, frame_mod, maps)


def home_kernel(scal, got, stream, frames, frame_mod, maps, out, xs, frame_row):
    section = scal[0]
    frame_row[0:1, 0:TOK] = frames[...].astype(F32)
    square = jnp.zeros((TOK, 128), F32)
    for head in range(HEADS):
        cols = slice(128 * head, 128 * head + 128)
        parts = [got[place_of(head, third)].astype(F32)[0:THIRD] for third in range(3)]
        x = jnp.where(section == 0, stream[:, cols].astype(F32), jnp.concatenate(parts, axis=0))
        xs[:, cols] = x
        square = square + x * x
    r = lax.rsqrt(jnp.sum(square, axis=1, keepdims=True) * (1.0 / WIDTH) + EPSILON)
    row = lax.broadcasted_iota(jnp.int32, (48, 128), 0)
    hot = jnp.where((row & 15).astype(F32) == frame_row[0:1, :], 1.0, 0.0).astype(BF16)
    for head in range(HEADS):
        cols = slice(128 * head, 128 * head + 128)
        more = slice(WIDTH + 128 * head, WIDTH + 128 * head + 128)
        mod = jnp.concatenate([frame_mod[:, cols], frame_mod[:, more]], axis=1)
        m = dot(hot, jnp.concatenate(split3(mod), axis=0).astype(BF16), TN)[0:TOK]
        hid = xs[:, cols] * r * (1.0 + m[:, 128:256]) + m[:, 0:128]
        out[0, :, cols] = (hid * maps[1:2, cols]).astype(BF16)
        out[1, :, cols] = (hid * maps[2:3, cols]).astype(BF16)


def home(section, got, stream, frames, frame_mod, maps):
    whole = pl.BlockSpec(memory_space=pltpu.VMEM)
    return pl.pallas_call(
        home_kernel,
        in_specs=[pl.BlockSpec(memory_space=pltpu.SMEM)] + [whole] * 5,
        out_specs=whole,
        out_shape=jax.ShapeDtypeStruct((2, TOK, WIDTH), BF16),
        scratch_shapes=[pltpu.VMEM((TOK, WIDTH), F32), pltpu.VMEM((8, 128), F32)],
        compiler_params=PARAMS,
        name="home",
    )(section, got, stream, frames, frame_mod, maps)


def mix_kernel(scal, mine, other, out):
    branch = scal[0]
    for t in range(PATCHES // 2):
        a = mine[80 * t : 80 * t + 80, :].astype(F32)
        b = other[80 * t : 80 * t + 80, :].astype(F32)
        cond, uncond = jnp.where(branch == 0, a, b), jnp.where(branch == 0, b, a)
        guided = uncond + GUIDE * (cond - uncond)
        for half in range(2):
            block = guided[THIRD * half : THIRD * half + THIRD].astype(BF16)
            out[2 * t + half] = block
            out[PATCHES + 2 * t + half] = block


def mix(branch, mine, other):
    whole = pl.BlockSpec(memory_space=pltpu.VMEM)
    return pl.pallas_call(
        mix_kernel,
        in_specs=[pl.BlockSpec(memory_space=pltpu.SMEM), whole, whole],
        out_specs=whole,
        out_shape=jax.ShapeDtypeStruct((64, THIRD, 128), BF16),
        compiler_params=PARAMS,
        name="mix",
    )(branch, mine, other)


def unpack_kernel(scal, got, out):
    branch = scal[0]
    for j in range(HEADS // 2):
        parts = []
        for third in range(3):
            a, b = place_of(j, third), place_of(j + HEADS // 2, third)
            parts.append(got[jnp.where(branch == 0, a, b)].astype(F32))
        out[:, 128 * j : 128 * j + 128] = jnp.concatenate(parts, axis=0).astype(BF16)


def unpack(branch, got):
    whole = pl.BlockSpec(memory_space=pltpu.VMEM)
    return pl.pallas_call(
        unpack_kernel,
        in_specs=[pl.BlockSpec(memory_space=pltpu.SMEM), whole],
        out_specs=whole,
        out_shape=jax.ShapeDtypeStruct((TOK, WIDTH // 2), BF16),
        compiler_params=PARAMS,
        name="unpack",
    )(branch, got)


def body(stream, token_frame, frame_levels, level_table, branch_mod, layer_mod, maps, stale_kv):
    section = lax.axis_index("section")
    branch = lax.axis_index("branch")
    place = section * PATCHES + lax.axis_index("patch")
    x, y, z = place % 4, (place // 4) % 4, place // 16
    head = jnp.where(x < 3, place // 4, 16 + z)
    third = jnp.where(x < 3, x, jnp.where(y < 3, y, 0))

    both = jnp.concatenate([layer_mod.reshape(3, WIDTH), maps[0]], axis=0)
    other = lax.ppermute(both, "section", [(0, 1), (1, 0)])

    frames = token_frame.reshape(1, TOK)
    section_at = section.reshape(1).astype(jnp.int32)
    send = pack(section_at, stale_kv[0, 0], stream, frames)
    received = lax.all_to_all(send, PLANE, 0, 0, tiled=True)
    received = received.reshape(2, PATCHES, CHUNK, 128)

    level_hot = (frame_levels[:, None] == jnp.arange(LEVELS, dtype=jnp.int32)[None, :]).astype(F32)
    base = jnp.dot(level_hot, level_table, precision=lax.Precision.HIGHEST, preferred_element_type=F32)
    home_mod = base + (layer_mod[0] + branch_mod[0])[None, :]

    def of_head(array):
        rows = array.shape[0]
        return lax.dynamic_slice_in_dim(array.reshape(rows, -1, HEADS, 128), head, 1, 2)[:, :, 0]

    layers = jnp.stack([jnp.where(section == 0, both, other), jnp.where(section == 0, other, both)])
    mine = of_head(layers.reshape(12, WIDTH)).reshape(2, 6, 128)
    base_mine = of_head(base)
    branch_mine = of_head(branch_mod)[0]
    mods = base_mine[None] + (mine[:, 0:3] + branch_mine[None])[:, None]
    mods = mods.reshape(2, FRAMES, 384)
    gains = mine[:, 3:6]

    x_one, mid = first_layer(received, mods[0], gains[0])

    def from_third(by):
        pairs = [(place_of(h, (g + by) % 3), place_of(h, g)) for h in range(HEADS) for g in range(3)]
        return lax.ppermute(x_one, PLANE, pairs)

    after, before = from_third(1), from_third(2)
    mid_got = lax.all_to_all(mid, PLANE, 0, 0, tiled=True)
    fresh = home(section_at, mid_got, stream, frames, home_mod, maps[0])
    x_two = second_layer(third.reshape(1).astype(jnp.int32), received, x_one, after, before, mid_got, mods[1], gains[1])

    x_other = lax.ppermute(x_two, "branch", [(0, 1), (1, 0)])
    branch_at = branch.reshape(1).astype(jnp.int32)
    guided = mix(branch_at, x_two, x_other)
    guided_got = lax.all_to_all(guided, PLANE, 0, 0, tiled=True)
    out = unpack(branch_at, guided_got)
    return (out, fresh[None, None])


def solution(mesh):
    placed = (
        P("patch", None),
        P("patch"),
        P(),
        P(),
        P("branch", None),
        P("section", None),
        P("section", None, None),
        P("branch", "section", None, "patch", None),
    )
    return jax.shard_map(
        body,
        mesh=mesh,
        in_specs=placed,
        out_specs=(P("patch", "branch"), P("branch", "section", None, "patch", None)),
        check_vma=False,
    )
```

```python
import functools
import math

import jax
import jax.numpy as jnp
from jax import lax
from jax.experimental import pallas as pl
from jax.experimental.pallas import tpu as pltpu
from jax.sharding import PartitionSpec as P

HEADS = 20
HEAD_DIM = 128
FRAMES = 16
LEVELS = 50
TOK = 120
THIRD = 40
PATCHES = 32
WIDTH = HEADS * HEAD_DIM
EPSILON = 1e-06
GUIDE = 5.0
BIG = 1e30
PLANE = ("section", "patch")
F32 = jnp.float32
BF16 = jnp.bfloat16
VMEM_BYTES = 56 * 1024 * 1024
PARAMS = pltpu.CompilerParams(vmem_limit_bytes=VMEM_BYTES)

OWN_ROWS = PATCHES * THIRD
TILE = 640
WIDE = 1280
SMALL = 1e-25
FACTOR = HEAD_DIM ** (-0.5) * math.log2(math.e)
CHUNK = 320
MID = 64


def place_of(head, third):
    if head < 16:
        return 4 * head + third
    return 16 * (head - 16) + 4 * third + 3


def dot(a, b, dims):
    return lax.dot_general(a, b, (dims, ((), ())), preferred_element_type=F32)


def block(shape):
    return pl.BlockSpec(shape, lambda i: (0,) * len(shape))


NN = ((1,), (0,))
NT = ((1,), (1,))
TN = ((0,), (0,))


def split3(v):
    hi = v.astype(BF16).astype(F32)
    mid = (v - hi).astype(BF16).astype(F32)
    low = (v - hi - mid).astype(BF16).astype(F32)
    return hi, mid, low


def turned(rows, third):
    cut = THIRD * third
    return rows if cut == 0 else jnp.concatenate([rows[cut:TOK], rows[:cut]], axis=0)


def pack_kernel(scal, stale, stream, frames, out, aux, frame_row):
    step = pl.program_id(0)
    section = scal[0]

    @pl.when(step == 0)
    def _():
        frame_row[...] = jnp.zeros((8, 128), F32)
        frame_row[0:1, 0:TOK] = frames[...].astype(F32)
        square = jnp.zeros((TOK, 128), F32)
        for head in range(HEADS):
            part = stream[:, 128 * head : 128 * head + 128].astype(F32)
            square = square + part * part
        square = jnp.concatenate([square, jnp.zeros((8, 128), F32)], axis=0)
        total = jnp.sum(square.T, axis=0, keepdims=True)
        r = lax.rsqrt(total * (1.0 / WIDTH) + EPSILON)
        hi, mid, low = split3(jnp.broadcast_to(r, (8, 128)))
        row = lax.broadcasted_iota(jnp.int32, (8, 128), 0)
        lane = lax.broadcasted_iota(jnp.int32, (8, 128), 1)
        a = jnp.where(row == 0, hi, jnp.where(row == 1, mid, jnp.where(row == 2, low, 0.0)))
        a = jnp.where(row == 3, frame_row[0:1, :], a)
        a = jnp.where(lane < TOK, a, 0.0)
        aux[0] = a
        for third in range(1, 3):
            cut = THIRD * third
            t = jnp.where(lane < TOK - cut, pltpu.roll(a, 128 - cut, 1), pltpu.roll(a, TOK - cut, 1))
            aux[third] = jnp.where(lane < TOK, t, 0.0)

    none = jnp.zeros((8, 128), F32)

    def blocks(head):
        cols = pl.ds(pl.multiple_of(head * 128, 128), 128)
        keys = stale[0, :, cols].astype(F32)
        vals = jnp.concatenate([stale[1, :, cols].astype(F32), none], axis=0).T.astype(BF16)
        x = stream[:, cols].astype(F32)
        halves = []
        for third in range(3):
            t = turned(x, third)
            halves.append(jnp.where(section == 0, t[0:64], t[TOK - 64 : TOK]).astype(BF16))
        return keys, vals, halves

    def put(at, keys, vals, x, third):
        out[at, 0:128] = jnp.concatenate([keys, aux[third]], axis=0).astype(BF16)
        out[at, 128:256] = vals
        out[at, 256:CHUNK] = x

    more_keys, more_vals, more_x = blocks(16 + step)
    for y in range(4):
        keys, vals, halves = blocks(4 * step + y)
        for third in range(3):
            put(4 * y + third, keys, vals, halves[third], third)
        put(4 * y + 3, more_keys, more_vals, more_x[y % 3], y % 3)


def pack(section, stale, stream, frames):
    grid = pltpu.PrefetchScalarGridSpec(
        num_scalar_prefetch=1,
        grid=(4,),
        in_specs=[
            pl.BlockSpec((2, TOK, WIDTH), lambda r, s: (0, 0, 0)),
            pl.BlockSpec((TOK, WIDTH), lambda r, s: (0, 0)),
            pl.BlockSpec((1, TOK), lambda r, s: (0, 0)),
        ],
        out_specs=pl.BlockSpec((16, CHUNK, 128), lambda r, s: (r, 0, 0)),
        scratch_shapes=[pltpu.VMEM((3, 8, 128), F32), pltpu.VMEM((8, 128), F32)],
    )
    return pl.pallas_call(
        pack_kernel,
        grid_spec=grid,
        out_shape=jax.ShapeDtypeStruct((64, CHUNK, 128), BF16),
        compiler_params=PARAMS,
        name="pack",
    )(section, stale, stream, frames)


def mod_table(frame_mod, with_scale):
    hi, mid, low = split3(frame_mod)
    table = jnp.concatenate([hi, mid, low, jnp.zeros((16, frame_mod.shape[1]), F32)], axis=0)
    if with_scale:
        row = lax.broadcasted_iota(jnp.int32, (64, 128), 0)
        extra = jnp.where((row >= 48) & (row < 51), 1.0, 0.0)
        table = jnp.concatenate([table, extra], axis=1)
    return table.astype(BF16)


def hot_rows(aux):
    row = lax.broadcasted_iota(jnp.int32, (48, 128), 0)
    hot = jnp.where((row & 15).astype(F32) == aux[3:4, :], 1.0, 0.0)
    return jnp.concatenate([hot, aux, jnp.zeros((8, 128), F32)], axis=0).astype(BF16)


def modulations(kv, table, mods):
    for begin in range(0, PATCHES, 8):
        hot = [hot_rows(kv[0, p, 112:128, :].astype(F32)[8:16]) for p in range(begin, begin + 8)]
        at = slice(begin * 128, begin * 128 + 1024)
        mods[at, 0 : table.shape[1]] = dot(jnp.concatenate(hot, axis=1), table, TN)


def place_pair(t, hids, maps, kv, qa, ka, vt, kf, vh):
    row = lax.broadcasted_iota(jnp.int32, (80, 128), 0)
    col = lax.broadcasted_iota(jnp.int32, (80, 128), 1)
    patch = 2 * t + jnp.where(row >= THIRD, 1, 0)
    at = slice(t * 80, t * 80 + 80)
    q = jnp.concatenate([hid[0:THIRD] for hid in hids], axis=0) * maps[0:1, :]
    qa[at, 0:128] = q.astype(BF16)
    qa[at, 128:256] = jnp.where((col == patch) | (col == PATCHES), 1.0, 0.0).astype(BF16)
    row = lax.broadcasted_iota(jnp.int32, (128, 128), 0)
    col = lax.broadcasted_iota(jnp.int32, (128, 128), 1)
    for half in range(2):
        p = 2 * t + half
        at = slice(p * 128, p * 128 + 128)
        ka[at, 0:128] = kv[0, p, 0:128, :]
        hidden = (col == p) | ((col == PATCHES) & (row >= TOK))
        ka[at, 128:256] = jnp.where(hidden, -BIG, 0.0).astype(BF16)
        vt[0:128, at] = kv[0, p, 128:256, :]
        kf[at, 0:128] = (hids[half] * maps[1:2, :]).astype(BF16)
        hidden = (col <= PATCHES) & ((row >= TOK) | ((col != p) & (col < PATCHES)))
        kf[at, 128:256] = jnp.where(hidden, -BIG, 0.0).astype(BF16)
        vh[at, :] = (hids[half] * maps[2:3, :]).astype(BF16)


def turn_values(vh, vt, vf):
    row = lax.broadcasted_iota(jnp.int32, (128, 128), 0)
    col = lax.broadcasted_iota(jnp.int32, (128, 128), 1)
    unit = jnp.where(row == col, 1.0, 0.0).astype(BF16)
    for begin in range(0, PATCHES * 128, 1024):
        at = slice(begin, begin + 1024)
        vf[0:128, at] = dot(unit, vh[at, :], NT).astype(BF16)
    vt[128:144, :] = jnp.ones((16, PATCHES * 128), BF16)
    vf[128:144, :] = jnp.ones((16, PATCHES * 128), BF16)


def norms(ref):
    ones = jnp.ones((8, 128), BF16)
    parts = []
    for begin in range(0, ref.shape[0], 640 if ref.shape[0] % 1024 else 1024):
        at = slice(begin, begin + (640 if ref.shape[0] % 1024 else 1024))
        v = ref[at, 0:128].astype(F32)
        parts.append(dot(ones, (v * v).astype(BF16), NT))
    return jnp.concatenate(parts, axis=1) * 1.01


def attention(qa, ka, vt, kf, vf, xo, go, sc, pt, result):
    step = 512
    stale = PATCHES * 128
    keys = stale + step
    row = lax.broadcasted_iota(jnp.int32, (128, 256), 0)
    col = lax.broadcasted_iota(jnp.int32, (128, 256), 1)
    unit = jnp.where((row == col) | (row + 128 == col), 1.0, 0.0).astype(BF16)

    def fresh_at(lane):
        low = lane // TILE * (TILE // THIRD) + lane % TILE // 128 * 3
        return pl.ds(low * 128 if isinstance(low, int) else pl.multiple_of(low * 128, 128), step)

    def scores(first, width, begin):
        return dot(ka[pl.ds(begin, step), :], qa[pl.ds(first, width), :], NT)

    def fresh_scores(first, width):
        lanes = [first + i for i in range(0, width, 128)]
        parts = [dot(kf[fresh_at(lane), :], qa[pl.ds(lane, 128), :], NT) for lane in lanes]
        return jnp.concatenate(parts, axis=1)

    def weigh(first, width, begin, s, top):
        weights = jnp.exp2((s - top) * FACTOR).astype(BF16)
        pt[pl.ds(begin, step), pl.ds(first, width)] = weights

    def finish(first, width):
        total = dot(vt[...], pt[0:stale, pl.ds(first, width)], NN)
        lanes = [first + i for i in range(0, width, 128)]
        more = [dot(vf[:, fresh_at(lane)], pt[stale:keys, pl.ds(lane, 128)], NN) for lane in lanes]
        total = total + jnp.concatenate(more, axis=1)
        mean = total[0:128] / total[128:129]
        hi = mean.astype(BF16)
        low = (mean - hi.astype(F32)).astype(BF16)
        for i, lane in enumerate(lanes):
            cols = slice(128 * i, 128 * i + 128)
            attended = dot(unit, jnp.concatenate([hi[:, cols], low[:, cols]], axis=1), NT)
            at = pl.ds(lane, 128)
            result(at, (xo[at, :] + go[at, :] * attended).astype(BF16))
        return jnp.min(total[128:129])

    lane = lax.broadcasted_iota(jnp.int32, (8, stale), 1)
    longest = jnp.where((lane & 127) < TOK, jnp.maximum(norms(ka), norms(kf)), 0.0)
    longest = jnp.max(longest, axis=1, keepdims=True)[0:1]
    bound = jnp.sqrt(norms(qa)[0:1] * longest)
    least = None
    for first in range(0, OWN_ROWS, WIDE):
        top = bound[:, first : first + WIDE]
        for begin in range(0, stale, step):
            weigh(first, WIDE, begin, scores(first, WIDE, begin), top)
        weigh(first, WIDE, stale, fresh_scores(first, WIDE), top)
        here = finish(first, WIDE)
        least = here if least is None else jnp.minimum(least, here)

    @pl.when(jnp.logical_not(least > SMALL))
    def _():
        @pl.loop(0, OWN_ROWS // TILE)
        def _(tile):
            first = pl.multiple_of(tile * TILE, 128)
            s = fresh_scores(first, TILE)
            sc[stale:keys, :] = s

            def one(i, top):
                begin = pl.multiple_of(i * step, step)
                s = scores(first, TILE, begin)
                sc[pl.ds(begin, step), :] = s
                return jnp.maximum(top, jnp.max(s.reshape(step // 8, 8, TILE), axis=0))

            top = lax.fori_loop(0, stale // step, one, jnp.max(s.reshape(step // 8, 8, TILE), axis=0))
            top = jnp.max(top, axis=0, keepdims=True)

            @pl.loop(0, keys // step)
            def _(i):
                begin = pl.multiple_of(i * step, step)
                weigh(first, TILE, begin, sc[pl.ds(begin, step), :], top)

            finish(first, TILE)


def first_kernel(kv, x_rest, frame_mod, maps, x_out, mid, qa, ka, vt, kf, vf, xo, go, sc, pt, mods, vh, sq):
    table = mod_table(frame_mod[...], True)
    gains = maps[...]

    modulations(kv, table, mods)
    for t in range(PATCHES // 2):
        at = slice(t * 80, t * 80 + 80)
        hids, xs, gates = [], [], []
        for half in range(2):
            p = 2 * t + half
            xa = kv[0, p, 256:CHUNK, :].astype(F32)
            xb = x_rest[0, p].astype(F32)[8:64]
            x = jnp.concatenate([xa, xb, jnp.zeros((8, 128), F32)], axis=0)
            m = mods[p * 128 : p * 128 + 128, :]
            hids.append(x * m[:, 384:512] * (1.0 + m[:, 128:256]) + m[:, 0:128])
            xs.append(x[0:THIRD])
            gates.append(m[0:THIRD, 256:384])
        place_pair(t, hids, gains, kv, qa, ka, vt, kf, vh)
        xo[at, :] = jnp.concatenate(xs, axis=0)
        go[at, :] = jnp.concatenate(gates, axis=0)
    turn_values(vh, vt, vf)

    def result(at, value):
        x_out[at, :] = value
        wide = value.astype(F32)
        sq[at, :] = wide * wide

    attention(qa, ka, vt, kf, vf, xo, go, sc, pt, result)
    square = sq[...]
    hi = square.astype(BF16)
    low = (square - hi.astype(F32)).astype(BF16)
    ones = jnp.ones((8, 128), BF16)
    total = dot(ones, hi, NT) + dot(ones, low, NT)
    hi = total.astype(BF16).astype(F32)
    low = total - hi
    rows = [part[0:1, 128 * i : 128 * i + 128] for part in (hi, low) for i in range(10)]
    sums = jnp.concatenate(rows + [jnp.zeros((4, 128), F32)], axis=0)
    for t in range(PATCHES // 2):
        pair = x_out[80 * t : 80 * t + 80, :].astype(F32)
        for half in range(2):
            p = 2 * t + half
            block = jnp.concatenate([pair[THIRD * half : THIRD * half + THIRD], sums], axis=0).astype(BF16)
            mid[p] = block
            mid[PATCHES + p] = block


SCRATCH = [
    pltpu.VMEM((OWN_ROWS, 256), BF16),
    pltpu.VMEM((PATCHES * 128, 256), BF16),
    pltpu.VMEM((144, PATCHES * 128), BF16),
    pltpu.VMEM((PATCHES * 128, 256), BF16),
    pltpu.VMEM((144, PATCHES * 128), BF16),
    pltpu.VMEM((OWN_ROWS, 128), F32),
    pltpu.VMEM((OWN_ROWS, 128), F32),
    pltpu.VMEM((PATCHES * 128 + 512, TILE), F32),
    pltpu.VMEM((PATCHES * 128 + 512, OWN_ROWS), BF16),
    pltpu.VMEM((PATCHES * 128, 512), F32),
    pltpu.VMEM((PATCHES * 128, 128), BF16),
]


def first_layer(received, frame_mod, maps):
    return pl.pallas_call(
        first_kernel,
        grid=(1,),
        in_specs=[
            pl.BlockSpec((1, PATCHES, CHUNK, 128), lambda i: (0, 0, 0, 0)),
            pl.BlockSpec((1, PATCHES, 64, 128), lambda i: (1, 0, 4, 0)),
            pl.BlockSpec((16, 384), lambda i: (0, 0)),
            pl.BlockSpec((3, 128), lambda i: (0, 0)),
        ],
        out_specs=[
            pl.BlockSpec((OWN_ROWS, 128), lambda i: (0, 0)),
            pl.BlockSpec((64, MID, 128), lambda i: (0, 0, 0)),
        ],
        out_shape=[
            jax.ShapeDtypeStruct((OWN_ROWS, 128), BF16),
            jax.ShapeDtypeStruct((64, MID, 128), BF16),
        ],
        scratch_shapes=SCRATCH + [pltpu.VMEM((OWN_ROWS, 128), F32)],
        compiler_params=PARAMS,
        name="first_layer",
    )(received, received, frame_mod, maps)


def second_kernel(scal, kv, own, after, before, sums, frame_mod, maps, x_out, qa, ka, vt, kf, vf, xo, go, sc, pt, mods, vh, rs):
    table = mod_table(frame_mod[...], False)
    gains = maps[...]
    third = scal[0]
    row = lax.broadcasted_iota(jnp.int32, (16, OWN_ROWS), 0)
    ones = jnp.where(lax.broadcasted_iota(jnp.int32, (16, 128), 0) < 3, 1.0, 0.0).astype(BF16)
    for k in range(3):
        which = lax.rem(third + k, 3)
        total = None
        for head in range(HEADS):
            at = 4 * head + which if head < 16 else 16 * (head - 16) + 4 * which + 3
            part = sums[at].astype(F32)
            total = part if total is None else total + part
        square = jnp.concatenate([total[8 + i : 9 + i] + total[18 + i : 19 + i] for i in range(10)], axis=1)
        hi, mid, low = split3(lax.rsqrt(square * (1.0 / WIDTH) + EPSILON))
        r = jnp.where(row == 0, hi, jnp.where(row == 1, mid, jnp.where(row == 2, low, 0.0)))
        rs[k] = dot(r.astype(BF16), ones, TN)

    modulations(kv, table, mods)
    for t in range(PATCHES // 2):
        at = slice(t * 80, t * 80 + 80)
        pair = [ref[at, :].astype(F32) for ref in (own, after, before)]
        scale = [rs[k, at, :] for k in range(3)]
        hids, gates = [], []
        for half in range(2):
            p = 2 * t + half
            cut = slice(THIRD * half, THIRD * half + THIRD)
            none = [jnp.zeros((8, 128), F32)]
            x = jnp.concatenate([v[cut] for v in pair] + none, axis=0)
            r = jnp.concatenate([v[cut] for v in scale] + none, axis=0)
            m = mods[p * 128 : p * 128 + 128, 0:384]
            hids.append(x * r * (1.0 + m[:, 128:256]) + m[:, 0:128])
            gates.append(m[0:THIRD, 256:384])
        place_pair(t, hids, gains, kv, qa, ka, vt, kf, vh)
        xo[at, :] = pair[0]
        go[at, :] = jnp.concatenate(gates, axis=0)
    turn_values(vh, vt, vf)

    def result(at, value):
        x_out[at, :] = value

    attention(qa, ka, vt, kf, vf, xo, go, sc, pt, result)


def second_layer(third, received, own, after, before, sums, frame_mod, maps):
    rows = pl.BlockSpec((OWN_ROWS, 128), lambda i, s: (0, 0))
    grid = pltpu.PrefetchScalarGridSpec(
        num_scalar_prefetch=1,
        grid=(1,),
        in_specs=[
            pl.BlockSpec((1, PATCHES, 256, 128), lambda i, s: (1, 0, 0, 0)),
            rows,
            rows,
            rows,
            pl.BlockSpec((64, 32, 128), lambda i, s: (0, 1, 0)),
            pl.BlockSpec((16, 384), lambda i, s: (0, 0)),
            pl.BlockSpec((3, 128), lambda i, s: (0, 0)),
        ],
        out_specs=rows,
        scratch_shapes=SCRATCH + [pltpu.VMEM((3, OWN_ROWS, 128), F32)],
    )
    return pl.pallas_call(
        second_kernel,
        grid_spec=grid,
        out_shape=jax.ShapeDtypeStruct((OWN_ROWS, 128), BF16),
        compiler_params=PARAMS,
        name="second_layer",
    )(third, received, own, after, before, sums, frame_mod, maps)


def home_kernel(scal, got, stream, frames, frame_mod, maps, out, xs, frame_row):
    section = scal[0]
    frame_row[0:1, 0:TOK] = frames[...].astype(F32)
    square = jnp.zeros((TOK, 128), F32)
    for head in range(HEADS):
        cols = slice(128 * head, 128 * head + 128)
        parts = [got[place_of(head, third)].astype(F32)[0:THIRD] for third in range(3)]
        x = jnp.where(section == 0, stream[:, cols].astype(F32), jnp.concatenate(parts, axis=0))
        xs[:, cols] = x
        square = square + x * x
    r = lax.rsqrt(jnp.sum(square, axis=1, keepdims=True) * (1.0 / WIDTH) + EPSILON)
    row = lax.broadcasted_iota(jnp.int32, (48, 128), 0)
    hot = jnp.where((row & 15).astype(F32) == frame_row[0:1, :], 1.0, 0.0).astype(BF16)
    for head in range(HEADS):
        cols = slice(128 * head, 128 * head + 128)
        more = slice(WIDTH + 128 * head, WIDTH + 128 * head + 128)
        mod = jnp.concatenate([frame_mod[:, cols], frame_mod[:, more]], axis=1)
        m = dot(hot, jnp.concatenate(split3(mod), axis=0).astype(BF16), TN)[0:TOK]
        hid = xs[:, cols] * r * (1.0 + m[:, 128:256]) + m[:, 0:128]
        out[0, :, cols] = (hid * maps[1:2, cols]).astype(BF16)
        out[1, :, cols] = (hid * maps[2:3, cols]).astype(BF16)


def home(section, got, stream, frames, frame_mod, maps):
    operands = [got, stream, frames, frame_mod, maps]
    return pl.pallas_call(
        home_kernel,
        grid=(1,),
        in_specs=[pl.BlockSpec(memory_space=pltpu.SMEM)] + [block(v.shape) for v in operands],
        out_specs=block((2, TOK, WIDTH)),
        out_shape=jax.ShapeDtypeStruct((2, TOK, WIDTH), BF16),
        scratch_shapes=[pltpu.VMEM((TOK, WIDTH), F32), pltpu.VMEM((8, 128), F32)],
        compiler_params=PARAMS,
        name="home",
    )(section, got, stream, frames, frame_mod, maps)


def mix_kernel(scal, mine, other, out):
    branch = scal[0]
    for t in range(PATCHES // 2):
        a = mine[80 * t : 80 * t + 80, :].astype(F32)
        b = other[80 * t : 80 * t + 80, :].astype(F32)
        cond, uncond = jnp.where(branch == 0, a, b), jnp.where(branch == 0, b, a)
        guided = uncond + GUIDE * (cond - uncond)
        for half in range(2):
            block = guided[THIRD * half : THIRD * half + THIRD].astype(BF16)
            out[2 * t + half] = block
            out[PATCHES + 2 * t + half] = block


def mix(branch, mine, other):
    return pl.pallas_call(
        mix_kernel,
        grid=(1,),
        in_specs=[pl.BlockSpec(memory_space=pltpu.SMEM), block(mine.shape), block(other.shape)],
        out_specs=block((64, THIRD, 128)),
        out_shape=jax.ShapeDtypeStruct((64, THIRD, 128), BF16),
        compiler_params=PARAMS,
        name="mix",
    )(branch, mine, other)


def unpack_kernel(scal, got, out):
    branch = scal[0]
    for j in range(HEADS // 2):
        parts = []
        for third in range(3):
            a, b = place_of(j, third), place_of(j + HEADS // 2, third)
            parts.append(got[jnp.where(branch == 0, a, b)].astype(F32))
        out[:, 128 * j : 128 * j + 128] = jnp.concatenate(parts, axis=0).astype(BF16)


def unpack(branch, got):
    return pl.pallas_call(
        unpack_kernel,
        grid=(1,),
        in_specs=[pl.BlockSpec(memory_space=pltpu.SMEM), block(got.shape)],
        out_specs=block((TOK, WIDTH // 2)),
        out_shape=jax.ShapeDtypeStruct((TOK, WIDTH // 2), BF16),
        compiler_params=PARAMS,
        name="unpack",
    )(branch, got)


def body(stream, token_frame, frame_levels, level_table, branch_mod, layer_mod, maps, stale_kv):
    section = lax.axis_index("section")
    branch = lax.axis_index("branch")
    place = section * PATCHES + lax.axis_index("patch")
    x, y, z = place % 4, (place // 4) % 4, place // 16
    head = jnp.where(x < 3, place // 4, 16 + z)
    third = jnp.where(x < 3, x, jnp.where(y < 3, y, 0))

    both = jnp.concatenate([layer_mod.reshape(3, WIDTH), maps[0]], axis=0)
    other = lax.ppermute(both, "section", [(0, 1), (1, 0)])

    frames = token_frame.reshape(1, TOK)
    section_at = section.reshape(1).astype(jnp.int32)
    send = pack(section_at, stale_kv[0, 0], stream, frames)
    received = lax.all_to_all(send, PLANE, 0, 0, tiled=True)
    received = received.reshape(2, PATCHES, CHUNK, 128)

    level_hot = (frame_levels[:, None] == jnp.arange(LEVELS, dtype=jnp.int32)[None, :]).astype(F32)
    base = jnp.dot(level_hot, level_table, precision=lax.Precision.HIGHEST, preferred_element_type=F32)
    home_mod = base + (layer_mod[0] + branch_mod[0])[None, :]

    def of_head(array):
        rows = array.shape[0]
        return lax.dynamic_slice_in_dim(array.reshape(rows, -1, HEADS, 128), head, 1, 2)[:, :, 0]

    layers = jnp.stack([jnp.where(section == 0, both, other), jnp.where(section == 0, other, both)])
    mine = of_head(layers.reshape(12, WIDTH)).reshape(2, 6, 128)
    base_mine = of_head(base)
    branch_mine = of_head(branch_mod)[0]
    mods = base_mine[None] + (mine[:, 0:3] + branch_mine[None])[:, None]
    mods = mods.reshape(2, FRAMES, 384)
    gains = mine[:, 3:6]

    x_one, mid = first_layer(received, mods[0], gains[0])

    def from_third(by):
        pairs = [(place_of(h, (g + by) % 3), place_of(h, g)) for h in range(HEADS) for g in range(3)]
        return lax.ppermute(x_one, PLANE, pairs)

    after, before = from_third(1), from_third(2)
    mid_got = lax.all_to_all(mid, PLANE, 0, 0, tiled=True)
    fresh = home(section_at, mid_got, stream, frames, home_mod, maps[0])
    x_two = second_layer(third.reshape(1).astype(jnp.int32), received, x_one, after, before, mid_got, mods[1], gains[1])

    x_other = lax.ppermute(x_two, "branch", [(0, 1), (1, 0)])
    branch_at = branch.reshape(1).astype(jnp.int32)
    guided = mix(branch_at, x_two, x_other)
    guided_got = lax.all_to_all(guided, PLANE, 0, 0, tiled=True)
    out = unpack(branch_at, guided_got)
    return (out, fresh[None, None])


def solution(mesh):
    placed = (
        P("patch", None),
        P("patch"),
        P(),
        P(),
        P("branch", None),
        P("section", None),
        P("section", None, None),
        P("branch", "section", None, "patch", None),
    )
    return jax.shard_map(
        body,
        mesh=mesh,
        in_specs=placed,
        out_specs=(P("patch", "branch"), P("branch", "section", None, "patch", None)),
        check_vma=False,
    )
```

```python
import functools
import math

import jax
import jax.numpy as jnp
from jax import lax
from jax.experimental import pallas as pl
from jax.experimental.pallas import tpu as pltpu
from jax.sharding import PartitionSpec as P

HEADS = 20
HEAD_DIM = 128
FRAMES = 16
LEVELS = 50
TOK = 120
THIRD = 40
PATCHES = 32
WIDTH = HEADS * HEAD_DIM
EPSILON = 1e-06
GUIDE = 5.0
BIG = 1e30
PLANE = ("section", "patch")
F32 = jnp.float32
BF16 = jnp.bfloat16
VMEM_BYTES = 56 * 1024 * 1024
PARAMS = pltpu.CompilerParams(vmem_limit_bytes=VMEM_BYTES)

OWN_ROWS = PATCHES * THIRD
TILE = 640
WIDE = 1280
SMALL = 1e-25
FACTOR = HEAD_DIM ** (-0.5) * math.log2(math.e)
CHUNK = 320
MID = 64


def place_of(head, third):
    if head < 16:
        return 4 * head + third
    return 16 * (head - 16) + 4 * third + 3


def dot(a, b, dims):
    return lax.dot_general(a, b, (dims, ((), ())), preferred_element_type=F32)


def block(shape):
    return pl.BlockSpec(shape, lambda i: (0,) * len(shape))


NN = ((1,), (0,))
NT = ((1,), (1,))
TN = ((0,), (0,))


def split3(v):
    hi = v.astype(BF16).astype(F32)
    mid = (v - hi).astype(BF16).astype(F32)
    low = (v - hi - mid).astype(BF16).astype(F32)
    return hi, mid, low


def turned(rows, third):
    cut = THIRD * third
    return rows if cut == 0 else jnp.concatenate([rows[cut:TOK], rows[:cut]], axis=0)


def pack_kernel(scal, stale, stream, frames, out, aux, frame_row):
    step = pl.program_id(0)
    section = scal[0]

    @pl.when(step == 0)
    def _():
        frame_row[...] = jnp.zeros((8, 128), F32)
        frame_row[0:1, 0:TOK] = frames[...].astype(F32)
        square = jnp.zeros((TOK, 128), F32)
        for head in range(HEADS):
            part = stream[:, 128 * head : 128 * head + 128].astype(F32)
            square = square + part * part
        square = jnp.concatenate([square, jnp.zeros((8, 128), F32)], axis=0)
        total = jnp.sum(square.T, axis=0, keepdims=True)
        r = lax.rsqrt(total * (1.0 / WIDTH) + EPSILON)
        hi, mid, low = split3(jnp.broadcast_to(r, (8, 128)))
        row = lax.broadcasted_iota(jnp.int32, (8, 128), 0)
        lane = lax.broadcasted_iota(jnp.int32, (8, 128), 1)
        a = jnp.where(row == 0, hi, jnp.where(row == 1, mid, jnp.where(row == 2, low, 0.0)))
        a = jnp.where(row == 3, frame_row[0:1, :], a)
        a = jnp.where(lane < TOK, a, 0.0)
        aux[0] = a
        for third in range(1, 3):
            cut = THIRD * third
            t = jnp.where(lane < TOK - cut, pltpu.roll(a, 128 - cut, 1), pltpu.roll(a, TOK - cut, 1))
            aux[third] = jnp.where(lane < TOK, t, 0.0)

    none = jnp.zeros((8, 128), F32)

    def blocks(head):
        cols = pl.ds(pl.multiple_of(head * 128, 128), 128)
        keys = stale[0, :, cols].astype(F32)
        vals = jnp.concatenate([stale[1, :, cols].astype(F32), none], axis=0).T.astype(BF16)
        x = stream[:, cols].astype(F32)
        halves = []
        for third in range(3):
            t = turned(x, third)
            halves.append(jnp.where(section == 0, t[0:64], t[TOK - 64 : TOK]).astype(BF16))
        return keys, vals, halves

    def put(at, keys, vals, x, third):
        out[at, 0:128] = jnp.concatenate([keys, aux[third]], axis=0).astype(BF16)
        out[at, 128:256] = vals
        out[at, 256:CHUNK] = x

    more_keys, more_vals, more_x = blocks(16 + step)
    for y in range(4):
        keys, vals, halves = blocks(4 * step + y)
        for third in range(3):
            put(4 * y + third, keys, vals, halves[third], third)
        put(4 * y + 3, more_keys, more_vals, more_x[y % 3], y % 3)


def pack(section, stale, stream, frames):
    grid = pltpu.PrefetchScalarGridSpec(
        num_scalar_prefetch=1,
        grid=(4,),
        in_specs=[
            pl.BlockSpec((2, TOK, WIDTH), lambda r, s: (0, 0, 0)),
            pl.BlockSpec((TOK, WIDTH), lambda r, s: (0, 0)),
            pl.BlockSpec((1, TOK), lambda r, s: (0, 0)),
        ],
        out_specs=pl.BlockSpec((16, CHUNK, 128), lambda r, s: (r, 0, 0)),
        scratch_shapes=[pltpu.VMEM((3, 8, 128), F32), pltpu.VMEM((8, 128), F32)],
    )
    return pl.pallas_call(
        pack_kernel,
        grid_spec=grid,
        out_shape=jax.ShapeDtypeStruct((64, CHUNK, 128), BF16),
        compiler_params=PARAMS,
        name="pack",
    )(section, stale, stream, frames)


def mod_table(frame_mod, with_scale):
    hi, mid, low = split3(frame_mod)
    table = jnp.concatenate([hi, mid, low, jnp.zeros((16, frame_mod.shape[1]), F32)], axis=0)
    if with_scale:
        row = lax.broadcasted_iota(jnp.int32, (64, 128), 0)
        extra = jnp.where((row >= 48) & (row < 51), 1.0, 0.0)
        table = jnp.concatenate([table, extra], axis=1)
    return table.astype(BF16)


def hot_rows(aux):
    row = lax.broadcasted_iota(jnp.int32, (48, 128), 0)
    hot = jnp.where((row & 15).astype(F32) == aux[3:4, :], 1.0, 0.0)
    return jnp.concatenate([hot, aux, jnp.zeros((8, 128), F32)], axis=0).astype(BF16)


def modulations(kv, table, mods):
    for begin in range(0, PATCHES, 8):
        hot = [hot_rows(kv[0, p, 112:128, :].astype(F32)[8:16]) for p in range(begin, begin + 8)]
        at = slice(begin * 128, begin * 128 + 1024)
        mods[at, 0 : table.shape[1]] = dot(jnp.concatenate(hot, axis=1), table, TN)


def place_pair(t, hids, maps, kv, qa, ka, vt, kf, vh):
    row = lax.broadcasted_iota(jnp.int32, (80, 128), 0)
    col = lax.broadcasted_iota(jnp.int32, (80, 128), 1)
    patch = 2 * t + jnp.where(row >= THIRD, 1, 0)
    at = slice(t * 80, t * 80 + 80)
    q = jnp.concatenate([hid[0:THIRD] for hid in hids], axis=0) * maps[0:1, :]
    qa[at, 0:128] = q.astype(BF16)
    qa[at, 128:256] = jnp.where((col == patch) | (col == PATCHES), 1.0, 0.0).astype(BF16)
    row = lax.broadcasted_iota(jnp.int32, (128, 128), 0)
    col = lax.broadcasted_iota(jnp.int32, (128, 128), 1)
    for half in range(2):
        p = 2 * t + half
        at = slice(p * 128, p * 128 + 128)
        ka[at, 0:128] = kv[0, p, 0:128, :]
        hidden = (col == p) | ((col == PATCHES) & (row >= TOK))
        ka[at, 128:256] = jnp.where(hidden, -BIG, 0.0).astype(BF16)
        vt[0:128, at] = kv[0, p, 128:256, :]
        kf[at, 0:128] = (hids[half] * maps[1:2, :]).astype(BF16)
        hidden = (col <= PATCHES) & ((row >= TOK) | ((col != p) & (col < PATCHES)))
        kf[at, 128:256] = jnp.where(hidden, -BIG, 0.0).astype(BF16)
        vh[at, :] = (hids[half] * maps[2:3, :]).astype(BF16)


def turn_values(vh, vt, vf):
    row = lax.broadcasted_iota(jnp.int32, (128, 128), 0)
    col = lax.broadcasted_iota(jnp.int32, (128, 128), 1)
    unit = jnp.where(row == col, 1.0, 0.0).astype(BF16)
    for begin in range(0, PATCHES * 128, 1024):
        at = slice(begin, begin + 1024)
        vf[0:128, at] = dot(unit, vh[at, :], NT).astype(BF16)
    vt[128:144, :] = jnp.ones((16, PATCHES * 128), BF16)
    vf[128:144, :] = jnp.ones((16, PATCHES * 128), BF16)


def norms(ref):
    ones = jnp.ones((8, 128), BF16)
    parts = []
    for begin in range(0, ref.shape[0], 640 if ref.shape[0] % 1024 else 1024):
        at = slice(begin, begin + (640 if ref.shape[0] % 1024 else 1024))
        v = ref[at, 0:128].astype(F32)
        parts.append(dot(ones, (v * v).astype(BF16), NT))
    return jnp.concatenate(parts, axis=1) * 1.01


def attention(qa, ka, vt, kf, vf, xo, go, sc, pt, result):
    step = 512
    stale = PATCHES * 128
    keys = stale + step
    row = lax.broadcasted_iota(jnp.int32, (128, 256), 0)
    col = lax.broadcasted_iota(jnp.int32, (128, 256), 1)
    unit = jnp.where((row == col) | (row + 128 == col), 1.0, 0.0).astype(BF16)

    def fresh_at(lane):
        low = lane // TILE * (TILE // THIRD) + lane % TILE // 128 * 3
        return pl.ds(low * 128 if isinstance(low, int) else pl.multiple_of(low * 128, 128), step)

    def scores(first, width, begin):
        return dot(ka[pl.ds(begin, step), :], qa[pl.ds(first, width), :], NT)

    def fresh_scores(first, width):
        lanes = [first + i for i in range(0, width, 128)]
        parts = [dot(kf[fresh_at(lane), :], qa[pl.ds(lane, 128), :], NT) for lane in lanes]
        return jnp.concatenate(parts, axis=1)

    def weigh(first, width, begin, s, top):
        weights = jnp.exp2((s - top) * FACTOR).astype(BF16)
        pt[pl.ds(begin, step), pl.ds(first, width)] = weights

    def finish(first, width):
        total = dot(vt[...], pt[0:stale, pl.ds(first, width)], NN)
        lanes = [first + i for i in range(0, width, 128)]
        more = [dot(vf[:, fresh_at(lane)], pt[stale:keys, pl.ds(lane, 128)], NN) for lane in lanes]
        total = total + jnp.concatenate(more, axis=1)
        mean = total[0:128] / total[128:129]
        hi = mean.astype(BF16)
        low = (mean - hi.astype(F32)).astype(BF16)
        for i, lane in enumerate(lanes):
            cols = slice(128 * i, 128 * i + 128)
            attended = dot(unit, jnp.concatenate([hi[:, cols], low[:, cols]], axis=1), NT)
            at = pl.ds(lane, 128)
            result(at, (xo[at, :] + go[at, :] * attended).astype(BF16))
        return jnp.min(total[128:129])

    lane = lax.broadcasted_iota(jnp.int32, (8, stale), 1)
    longest = jnp.where((lane & 127) < TOK, jnp.maximum(norms(ka), norms(kf)), 0.0)
    longest = jnp.max(longest, axis=1, keepdims=True)[0:1]
    bound = jnp.sqrt(norms(qa)[0:1] * longest)
    least = None
    for first in range(0, OWN_ROWS, WIDE):
        top = bound[:, first : first + WIDE]
        for begin in range(0, stale, step):
            weigh(first, WIDE, begin, scores(first, WIDE, begin), top)
        weigh(first, WIDE, stale, fresh_scores(first, WIDE), top)
        here = finish(first, WIDE)
        least = here if least is None else jnp.minimum(least, here)

    @pl.when(jnp.logical_not(least > SMALL))
    def _():
        @pl.loop(0, OWN_ROWS // TILE)
        def _(tile):
            first = pl.multiple_of(tile * TILE, 128)
            s = fresh_scores(first, TILE)
            sc[stale:keys, :] = s

            def one(i, top):
                begin = pl.multiple_of(i * step, step)
                s = scores(first, TILE, begin)
                sc[pl.ds(begin, step), :] = s
                return jnp.maximum(top, jnp.max(s.reshape(step // 8, 8, TILE), axis=0))

            top = lax.fori_loop(0, stale // step, one, jnp.max(s.reshape(step // 8, 8, TILE), axis=0))
            top = jnp.max(top, axis=0, keepdims=True)

            @pl.loop(0, keys // step)
            def _(i):
                begin = pl.multiple_of(i * step, step)
                weigh(first, TILE, begin, sc[pl.ds(begin, step), :], top)

            finish(first, TILE)


def first_kernel(kv, x_rest, frame_mod, maps, x_out, mid, qa, ka, vt, kf, vf, xo, go, sc, pt, mods, vh, sq):
    table = mod_table(frame_mod[...], True)
    gains = maps[...]

    modulations(kv, table, mods)
    for t in range(PATCHES // 2):
        at = slice(t * 80, t * 80 + 80)
        hids, xs, gates = [], [], []
        for half in range(2):
            p = 2 * t + half
            xa = kv[0, p, 256:CHUNK, :].astype(F32)
            xb = x_rest[0, p].astype(F32)[8:64]
            x = jnp.concatenate([xa, xb, jnp.zeros((8, 128), F32)], axis=0)
            m = mods[p * 128 : p * 128 + 128, :]
            hids.append(x * m[:, 384:512] * (1.0 + m[:, 128:256]) + m[:, 0:128])
            xs.append(x[0:THIRD])
            gates.append(m[0:THIRD, 256:384])
        place_pair(t, hids, gains, kv, qa, ka, vt, kf, vh)
        xo[at, :] = jnp.concatenate(xs, axis=0)
        go[at, :] = jnp.concatenate(gates, axis=0)
    turn_values(vh, vt, vf)

    def result(at, value):
        x_out[at, :] = value
        wide = value.astype(F32)
        sq[at, :] = wide * wide

    attention(qa, ka, vt, kf, vf, xo, go, sc, pt, result)
    square = sq[...]
    hi = square.astype(BF16)
    low = (square - hi.astype(F32)).astype(BF16)
    ones = jnp.ones((8, 128), BF16)
    total = dot(ones, hi, NT) + dot(ones, low, NT)
    hi = total.astype(BF16).astype(F32)
    low = total - hi
    rows = [part[0:1, 128 * i : 128 * i + 128] for part in (hi, low) for i in range(10)]
    sums = jnp.concatenate(rows + [jnp.zeros((4, 128), F32)], axis=0)
    for t in range(PATCHES // 2):
        pair = x_out[80 * t : 80 * t + 80, :].astype(F32)
        for half in range(2):
            p = 2 * t + half
            block = jnp.concatenate([pair[THIRD * half : THIRD * half + THIRD], sums], axis=0).astype(BF16)
            mid[p] = block
            mid[PATCHES + p] = block


SCRATCH = [
    pltpu.VMEM((OWN_ROWS, 256), BF16),
    pltpu.VMEM((PATCHES * 128, 256), BF16),
    pltpu.VMEM((144, PATCHES * 128), BF16),
    pltpu.VMEM((PATCHES * 128, 256), BF16),
    pltpu.VMEM((144, PATCHES * 128), BF16),
    pltpu.VMEM((OWN_ROWS, 128), F32),
    pltpu.VMEM((OWN_ROWS, 128), F32),
    pltpu.VMEM((PATCHES * 128 + 512, TILE), F32),
    pltpu.VMEM((PATCHES * 128 + 512, OWN_ROWS), BF16),
    pltpu.VMEM((PATCHES * 128, 512), F32),
    pltpu.VMEM((PATCHES * 128, 128), BF16),
]


def first_layer(received, frame_mod, maps):
    return pl.pallas_call(
        first_kernel,
        grid=(1,),
        in_specs=[
            pl.BlockSpec((1, PATCHES, CHUNK, 128), lambda i: (0, 0, 0, 0)),
            pl.BlockSpec((1, PATCHES, 64, 128), lambda i: (1, 0, 4, 0)),
            pl.BlockSpec((16, 384), lambda i: (0, 0)),
            pl.BlockSpec((3, 128), lambda i: (0, 0)),
        ],
        out_specs=[
            pl.BlockSpec((OWN_ROWS, 128), lambda i: (0, 0)),
            pl.BlockSpec((64, MID, 128), lambda i: (0, 0, 0)),
        ],
        out_shape=[
            jax.ShapeDtypeStruct((OWN_ROWS, 128), BF16),
            jax.ShapeDtypeStruct((64, MID, 128), BF16),
        ],
        scratch_shapes=SCRATCH + [pltpu.VMEM((OWN_ROWS, 128), F32)],
        compiler_params=PARAMS,
        name="first_layer",
    )(received, received, frame_mod, maps)


def second_kernel(scal, kv, own, after, before, sums, frame_mod, maps, x_out, qa, ka, vt, kf, vf, xo, go, sc, pt, mods, vh, rs):
    table = mod_table(frame_mod[...], False)
    gains = maps[...]
    third = scal[0]
    row = lax.broadcasted_iota(jnp.int32, (16, OWN_ROWS), 0)
    ones = jnp.where(lax.broadcasted_iota(jnp.int32, (16, 128), 0) < 3, 1.0, 0.0).astype(BF16)
    for k in range(3):
        which = lax.rem(third + k, 3)
        total = None
        for head in range(HEADS):
            at = 4 * head + which if head < 16 else 16 * (head - 16) + 4 * which + 3
            part = sums[at].astype(F32)
            total = part if total is None else total + part
        square = jnp.concatenate([total[8 + i : 9 + i] + total[18 + i : 19 + i] for i in range(10)], axis=1)
        hi, mid, low = split3(lax.rsqrt(square * (1.0 / WIDTH) + EPSILON))
        r = jnp.where(row == 0, hi, jnp.where(row == 1, mid, jnp.where(row == 2, low, 0.0)))
        rs[k] = dot(r.astype(BF16), ones, TN)

    modulations(kv, table, mods)
    for t in range(PATCHES // 2):
        at = slice(t * 80, t * 80 + 80)
        pair = [ref[at, :].astype(F32) for ref in (own, after, before)]
        scale = [rs[k, at, :] for k in range(3)]
        hids, gates = [], []
        for half in range(2):
            p = 2 * t + half
            cut = slice(THIRD * half, THIRD * half + THIRD)
            none = [jnp.zeros((8, 128), F32)]
            x = jnp.concatenate([v[cut] for v in pair] + none, axis=0)
            r = jnp.concatenate([v[cut] for v in scale] + none, axis=0)
            m = mods[p * 128 : p * 128 + 128, 0:384]
            hids.append(x * r * (1.0 + m[:, 128:256]) + m[:, 0:128])
            gates.append(m[0:THIRD, 256:384])
        place_pair(t, hids, gains, kv, qa, ka, vt, kf, vh)
        xo[at, :] = pair[0]
        go[at, :] = jnp.concatenate(gates, axis=0)
    turn_values(vh, vt, vf)

    def result(at, value):
        x_out[at, :] = value

    attention(qa, ka, vt, kf, vf, xo, go, sc, pt, result)


def second_layer(third, received, own, after, before, sums, frame_mod, maps):
    rows = pl.BlockSpec((OWN_ROWS, 128), lambda i, s: (0, 0))
    grid = pltpu.PrefetchScalarGridSpec(
        num_scalar_prefetch=1,
        grid=(1,),
        in_specs=[
            pl.BlockSpec((1, PATCHES, 256, 128), lambda i, s: (1, 0, 0, 0)),
            rows,
            rows,
            rows,
            pl.BlockSpec((64, 32, 128), lambda i, s: (0, 1, 0)),
            pl.BlockSpec((16, 384), lambda i, s: (0, 0)),
            pl.BlockSpec((3, 128), lambda i, s: (0, 0)),
        ],
        out_specs=rows,
        scratch_shapes=SCRATCH + [pltpu.VMEM((3, OWN_ROWS, 128), F32)],
    )
    return pl.pallas_call(
        second_kernel,
        grid_spec=grid,
        out_shape=jax.ShapeDtypeStruct((OWN_ROWS, 128), BF16),
        compiler_params=PARAMS,
        name="second_layer",
    )(third, received, own, after, before, sums, frame_mod, maps)


def home_kernel(scal, got, stream, frames, frame_mod, maps, out, xs, frame_row):
    section = scal[0]
    frame_row[0:1, 0:TOK] = frames[...].astype(F32)
    square = jnp.zeros((TOK, 128), F32)
    for head in range(HEADS):
        cols = slice(128 * head, 128 * head + 128)
        parts = [got[place_of(head, third)].astype(F32)[0:THIRD] for third in range(3)]
        x = jnp.where(section == 0, stream[:, cols].astype(F32), jnp.concatenate(parts, axis=0))
        xs[:, cols] = x
        square = square + x * x
    r = lax.rsqrt(jnp.sum(square, axis=1, keepdims=True) * (1.0 / WIDTH) + EPSILON)
    row = lax.broadcasted_iota(jnp.int32, (48, 128), 0)
    hot = jnp.where((row & 15).astype(F32) == frame_row[0:1, :], 1.0, 0.0).astype(BF16)
    for head in range(HEADS):
        cols = slice(128 * head, 128 * head + 128)
        more = slice(WIDTH + 128 * head, WIDTH + 128 * head + 128)
        mod = jnp.concatenate([frame_mod[:, cols], frame_mod[:, more]], axis=1)
        m = dot(hot, jnp.concatenate(split3(mod), axis=0).astype(BF16), TN)[0:TOK]
        hid = xs[:, cols] * r * (1.0 + m[:, 128:256]) + m[:, 0:128]
        out[0, :, cols] = (hid * maps[1:2, cols]).astype(BF16)
        out[1, :, cols] = (hid * maps[2:3, cols]).astype(BF16)


def home(section, got, stream, frames, frame_mod, maps):
    operands = [got, stream, frames, frame_mod, maps]
    return pl.pallas_call(
        home_kernel,
        grid=(1,),
        in_specs=[pl.BlockSpec(memory_space=pltpu.SMEM)] + [block(v.shape) for v in operands],
        out_specs=block((2, TOK, WIDTH)),
        out_shape=jax.ShapeDtypeStruct((2, TOK, WIDTH), BF16),
        scratch_shapes=[pltpu.VMEM((TOK, WIDTH), F32), pltpu.VMEM((8, 128), F32)],
        compiler_params=PARAMS,
        name="home",
    )(section, got, stream, frames, frame_mod, maps)


def mix_kernel(scal, mine, other, out):
    branch = scal[0]
    for t in range(4):
        a = mine[80 * t : 80 * t + 80, :].astype(F32)
        b = other[80 * t : 80 * t + 80, :].astype(F32)
        cond, uncond = jnp.where(branch == 0, a, b), jnp.where(branch == 0, b, a)
        guided = uncond + GUIDE * (cond - uncond)
        for half in range(2):
            block = guided[THIRD * half : THIRD * half + THIRD].astype(BF16)
            out[0, 2 * t + half] = block
            out[1, 2 * t + half] = block


def mix(branch, mine, other):
    rows = pl.BlockSpec((8 * THIRD, 128), lambda i: (i, 0))
    return pl.pallas_call(
        mix_kernel,
        grid=(PATCHES // 8,),
        in_specs=[pl.BlockSpec(memory_space=pltpu.SMEM), rows, rows],
        out_specs=pl.BlockSpec((2, 8, THIRD, 128), lambda i: (0, i, 0, 0)),
        out_shape=jax.ShapeDtypeStruct((2, PATCHES, THIRD, 128), BF16),
        compiler_params=PARAMS,
        name="mix",
    )(branch, mine, other)


def unpack_kernel(scal, got, out):
    branch = scal[0]
    for j in range(HEADS // 2):
        parts = []
        for third in range(3):
            a, b = place_of(j, third), place_of(j + HEADS // 2, third)
            parts.append(got[jnp.where(branch == 0, a, b)].astype(F32))
        out[:, 128 * j : 128 * j + 128] = jnp.concatenate(parts, axis=0).astype(BF16)


def unpack(branch, got):
    return pl.pallas_call(
        unpack_kernel,
        grid=(1,),
        in_specs=[pl.BlockSpec(memory_space=pltpu.SMEM), block(got.shape)],
        out_specs=block((TOK, WIDTH // 2)),
        out_shape=jax.ShapeDtypeStruct((TOK, WIDTH // 2), BF16),
        compiler_params=PARAMS,
        name="unpack",
    )(branch, got)


def body(stream, token_frame, frame_levels, level_table, branch_mod, layer_mod, maps, stale_kv):
    section = lax.axis_index("section")
    branch = lax.axis_index("branch")
    place = section * PATCHES + lax.axis_index("patch")
    x, y, z = place % 4, (place // 4) % 4, place // 16
    head = jnp.where(x < 3, place // 4, 16 + z)
    third = jnp.where(x < 3, x, jnp.where(y < 3, y, 0))

    both = jnp.concatenate([layer_mod.reshape(3, WIDTH), maps[0]], axis=0)
    other = lax.ppermute(both, "section", [(0, 1), (1, 0)])

    frames = token_frame.reshape(1, TOK)
    section_at = section.reshape(1).astype(jnp.int32)
    send = pack(section_at, stale_kv[0, 0], stream, frames)
    received = lax.all_to_all(send, PLANE, 0, 0, tiled=True)
    received = received.reshape(2, PATCHES, CHUNK, 128)

    level_hot = (frame_levels[:, None] == jnp.arange(LEVELS, dtype=jnp.int32)[None, :]).astype(F32)
    base = jnp.dot(level_hot, level_table, precision=lax.Precision.HIGHEST, preferred_element_type=F32)
    home_mod = base + (layer_mod[0] + branch_mod[0])[None, :]

    def of_head(array):
        rows = array.shape[0]
        return lax.dynamic_slice_in_dim(array.reshape(rows, -1, HEADS, 128), head, 1, 2)[:, :, 0]

    layers = jnp.stack([jnp.where(section == 0, both, other), jnp.where(section == 0, other, both)])
    mine = of_head(layers.reshape(12, WIDTH)).reshape(2, 6, 128)
    base_mine = of_head(base)
    branch_mine = of_head(branch_mod)[0]
    mods = base_mine[None] + (mine[:, 0:3] + branch_mine[None])[:, None]
    mods = mods.reshape(2, FRAMES, 384)
    gains = mine[:, 3:6]

    x_one, mid = first_layer(received, mods[0], gains[0])

    def from_third(by):
        pairs = [(place_of(h, (g + by) % 3), place_of(h, g)) for h in range(HEADS) for g in range(3)]
        return lax.ppermute(x_one, PLANE, pairs)

    after, before = from_third(1), from_third(2)
    mid_got = lax.all_to_all(mid, PLANE, 0, 0, tiled=True)
    fresh = home(section_at, mid_got, stream, frames, home_mod, maps[0])
    x_two = second_layer(third.reshape(1).astype(jnp.int32), received, x_one, after, before, mid_got, mods[1], gains[1])

    x_other = lax.ppermute(x_two, "branch", [(0, 1), (1, 0)])
    branch_at = branch.reshape(1).astype(jnp.int32)
    guided = mix(branch_at, x_two, x_other).reshape(64, THIRD, 128)
    guided_got = lax.all_to_all(guided, PLANE, 0, 0, tiled=True)
    out = unpack(branch_at, guided_got)
    return (out, fresh[None, None])


def solution(mesh):
    placed = (
        P("patch", None),
        P("patch"),
        P(),
        P(),
        P("branch", None),
        P("section", None),
        P("section", None, None),
        P("branch", "section", None, "patch", None),
    )
    return jax.shard_map(
        body,
        mesh=mesh,
        in_specs=placed,
        out_specs=(P("patch", "branch"), P("branch", "section", None, "patch", None)),
        check_vma=False,
    )
```
